32 devices in a mesh: dp: 8 (over z, y), tensor: 4 (over x, core).
Axes of the slice: x: 2, y: 2, z: 4, core: 2. Of those that a mesh axis runs over, the one named last changes fastest.
Arguments:
- tokens: bfloat16 [4096, 8192], P('dp', 'tensor'), may hold values from -55 to 55, as said below
- cotangent: bfloat16 [4096, 8192], P('dp', 'tensor'), may hold values from -1.1 to 1.1, as said below
- lowrank_down_factor: float32 [64, 8192], P(None, 'tensor'), may hold values from -0.22097087 to 0.22097087, as said below
- lowrank_up_factor: float32 [64, 8192], P(None, 'tensor'), may hold values from -0.22097087 to 0.22097087, as said below
- first_moment_estimate: float32 [2, 64, 8192], P(None, 'dp', 'tensor'), may hold values from -3 to 3
- second_moment_estimate: float32 [2, 64, 8192], P(None, 'dp', 'tensor'), may hold values from 0.02 to 0.5, as said below
Outputs:
- input_grad: bfloat16 [4096, 8192], P('dp', 'tensor')
- updated_down_factor: float32 [64, 8192], P('dp', 'tensor')
- updated_up_factor: float32 [64, 8192], P('dp', 'tensor')
- new_first: float32 [2, 64, 8192], P(None, 'dp', 'tensor')
- new_second: float32 [2, 64, 8192], P(None, 'dp', 'tensor')
The draws below stay inside these ranges and needn't reach their ends.
Inputs may be any that keep to these rules, and one draw needn't show every extreme that they name: `tokens`: bounded activations. `cotangent`: bounded gradients. `lowrank_down_factor`: bounded factor entries. `lowrank_up_factor`: bounded factor entries. `second_moment_estimate`: positive moments.
All inputs are finite; a program needn't handle non-finite values.
Results may differ from the reference program's by a relative error of at most 0.0063.
Values sent between devices are 32-bit elements; how exact they have to be, the bound alone decides.
No kernel may reach another device: no remote copies, remote signals or barrier semaphores. Data moves between devices by JAX's collectives and lax.ppermute only.
A program may use at most 64 MiB of HBM per device.

```python
import math
import jax
import jax.numpy as jnp
from jax import lax

D = 8192
R = 64
TOK_DEV = 512
TOKENS = 4096
LEVELS = 3
N_DP = 8


def mixed_rows(key, overall):
    key_shared, key_private, key_columns = jax.random.split(key, 3)
    shared = jnp.clip(jax.random.normal(key_shared, (TOK_DEV, D), jnp.float32), -4.0, 4.0)
    private = jnp.clip(jax.random.normal(key_private, (TOKENS, D), jnp.float32), -4.0, 4.0)
    weight_shared = 0.8
    weight_private = 0.6
    spread_log = math.log(10.0)
    column_scale = jnp.exp(spread_log * (jax.random.uniform(key_columns, (D,), jnp.float32) - 0.5))
    column_scale = column_scale * 3.0 ** (jnp.arange(D, dtype=jnp.float32) / D - 0.5)
    row_scale = 3.0 ** (jnp.arange(TOKENS, dtype=jnp.float32) / TOKENS - 0.5)
    mixture = weight_shared * jnp.tile(shared, (TOKENS // TOK_DEV, 1)) + weight_private * private
    return overall * mixture * row_scale[:, None] * column_scale[None, :]


def factor_rows(key):
    key_values, key_rows = jax.random.split(key, 2)
    values = jnp.clip(jax.random.normal(key_values, (R, D), jnp.float32), -4.0, 4.0)
    row_scale = jnp.exp(jax.random.uniform(key_rows, (R,), jnp.float32, math.log(0.3), math.log(3.0)))
    return values * row_scale[:, None] / math.sqrt(D)


def draw_tokens(key, part):
    return mixed_rows(jax.random.fold_in(key, 11), 1.0).astype(jnp.bfloat16)


def draw_cotangent(key, part):
    return mixed_rows(jax.random.fold_in(key, 12), 0.02).astype(jnp.bfloat16)


def draw_lowrank_down_factor(key, part):
    return factor_rows(jax.random.fold_in(key, 13))


def draw_lowrank_up_factor(key, part):
    return factor_rows(jax.random.fold_in(key, 14))


def draw_second_moment_estimate(key, part):
    moment_key = jax.random.fold_in(key, 15)
    lowest = TOK_DEV / 25600.0
    highest = TOK_DEV / 1024.0
    values = jnp.exp(jax.random.uniform(moment_key, (2, R, D), jnp.float32, math.log(lowest), math.log(highest)))
    return jnp.clip(values, lowest, highest)


def block_scale(key, extent, cuts, smallest, top_value):
    loudness, own = 1.0, jax.random.fold_in(key, 6)
    for axis_at, shards_of in cuts:
        heights = jnp.exp(jax.random.uniform(jax.random.fold_in(own, axis_at), (shards_of,), jnp.float32, smallest / len(cuts), top_value / len(cuts)))
        loudness = loudness * jnp.repeat(heights, extent[axis_at] // shards_of).reshape([-1 if axis == axis_at else 1 for axis in range(len(extent))])
    return loudness


def gaussian(rng, shape, scale, limit, cuts=(), held_as=jnp.bfloat16):
    level = block_scale(rng, shape, cuts, -0.22, 0.18) if cuts else 1.0
    values = jax.random.normal(rng, shape, jnp.float32) * scale * level
    return jnp.minimum(jnp.maximum(values, -limit), limit).astype(held_as)


def setup_inputs(seed: int = 0) -> dict:
    key_of = jax.random.split(jax.random.key(seed), 7)
    return {
        "tokens": draw_tokens(jax.random.fold_in(key_of[6], 71), 0),
        "cotangent": draw_cotangent(jax.random.fold_in(key_of[6], 71), 0),
        "lowrank_down_factor": draw_lowrank_down_factor(jax.random.fold_in(key_of[6], 71), 0),
        "lowrank_up_factor": draw_lowrank_up_factor(jax.random.fold_in(key_of[6], 71), 0),
        "first_moment_estimate": gaussian(key_of[4], (2, R, D), 0.5, 3.0, ((1, 8), (2, 4)), jnp.float32),
        "second_moment_estimate": draw_second_moment_estimate(jax.random.fold_in(key_of[6], 71), 0),
    }


SCALE = 2.0
NORM_EPS = 1e-06

def adapter_grads(row_block, cot_block, adapter_input_width, adapter_output_width):
    hidden = jnp.dot(row_block, adapter_input_width.T, preferred_element_type=jnp.float32).astype(jnp.bfloat16)
    upstream = jnp.dot(cot_block, adapter_output_width.T, preferred_element_type=jnp.float32).astype(jnp.bfloat16)
    dims = (((0,), (0,)), ((), ()))
    grad_a = SCALE * lax.dot_general(upstream, row_block, dims, preferred_element_type=jnp.float32)
    grad_b = SCALE * lax.dot_general(hidden, cot_block, dims, preferred_element_type=jnp.float32)
    input_part = (SCALE * jnp.dot(upstream, adapter_input_width, preferred_element_type=jnp.float32)).astype(jnp.bfloat16)
    return (jnp.stack([grad_a, grad_b]), input_part)

def adasum_pair(left_vec, right_vec):
    norm_left = lax.optimization_barrier(jnp.sum(left_vec * left_vec, -1))
    norm_right = lax.optimization_barrier(jnp.sum(right_vec * right_vec, -1))
    cross_term = lax.optimization_barrier(jnp.sum(left_vec * right_vec, -1))
    coef_left = 1.0 - cross_term / (2.0 * (norm_left + NORM_EPS))
    coef_right = 1.0 - cross_term / (2.0 * (norm_right + NORM_EPS))
    return coef_left[..., None] * left_vec + coef_right[..., None] * right_vec

def reference(tokens, cotangent, lowrank_down_factor, lowrank_up_factor, first_moment_estimate, second_moment_estimate):
    adapter_input_width = lowrank_down_factor.astype(jnp.bfloat16)
    adapter_output_width = lowrank_up_factor.astype(jnp.bfloat16)
    row_blocks = tokens.reshape(N_DP, TOK_DEV, D)
    cot_blocks = cotangent.reshape(N_DP, TOK_DEV, D)
    grads, input_parts = lax.map(lambda pieces: adapter_grads(pieces[0], pieces[1], adapter_input_width, adapter_output_width), (row_blocks, cot_blocks))
    vectors = grads.reshape(N_DP, 2, R * D)
    for level_index in range(LEVELS):
        vectors = adasum_pair(vectors[0::2], vectors[1::2])
    combined = vectors[0].reshape(2, R, D)
    moment_one = 0.9 * first_moment_estimate + 0.1 * combined
    moment_two = 0.95 * second_moment_estimate + 0.05 * combined * combined
    optimizer_update = 0.001 * moment_one / (jnp.sqrt(moment_two) + 1e-08)
    updated_down_factor = lowrank_down_factor - optimizer_update[0]
    updated_up_factor = lowrank_up_factor - optimizer_update[1]
    return (input_parts.reshape(TOKENS, D), updated_down_factor, updated_up_factor, moment_one, moment_two)
```

```python
import jax
import jax.numpy as jnp
from jax import lax
from jax.sharding import PartitionSpec as P

SCALE = 2.0
NORM_EPS = 1e-06


def butterfly_sum(block, axis):
    count = lax.axis_size(axis)
    apart = 1
    while apart < count:
        route = [(here, here ^ apart) for here in range(count)]
        block = block + lax.ppermute(block, axis, route)
        apart *= 2
    return block


def tree_weights(gram, levels):
    count = gram.shape[-1]
    index = jnp.arange(count)
    weights = jnp.ones(gram.shape[:-1], jnp.float32)
    for level in range(levels):
        group = index >> level
        same = (group[:, None] == group[None, :]).astype(jnp.float32)
        sibling = (group[:, None] == (group[None, :] ^ 1)).astype(jnp.float32)
        weighted = gram * weights[:, :, None] * weights[:, None, :]
        norm = jnp.sum(same * jnp.sum(same * weighted, -1)[:, None, :], -1)
        cross = jnp.sum(same * jnp.sum(sibling * weighted, -1)[:, None, :], -1)
        weights = weights * (1.0 - cross / (2.0 * (norm + NORM_EPS)))
    return weights


def body(
    tokens,
    cotangent,
    lowrank_down_factor,
    lowrank_up_factor,
    first_moment_estimate,
    second_moment_estimate,
):
    replicas = lax.axis_size("dp")
    everyone = replicas * lax.axis_size("tensor")
    levels = replicas.bit_length() - 1
    position = lax.axis_index("dp")
    rank, columns = lowrank_down_factor.shape
    owned_rows = first_moment_estimate.shape[1]
    adapter_in = lowrank_down_factor.astype(jnp.bfloat16)
    adapter_out = lowrank_up_factor.astype(jnp.bfloat16)
    contract_last = (((1,), (1,)), ((), ()))
    partial_sums = jnp.concatenate(
        [
            lax.dot_general(
                tokens, adapter_in, contract_last, preferred_element_type=jnp.float32
            ),
            lax.dot_general(
                cotangent, adapter_out, contract_last, preferred_element_type=jnp.float32
            ),
        ],
        1,
    )
    summed = SCALE * butterfly_sum(partial_sums, "tensor")
    hidden = summed[:, :rank].astype(jnp.bfloat16)
    upstream = summed[:, rank:].astype(jnp.bfloat16)
    input_grad = jnp.dot(upstream, adapter_in, preferred_element_type=jnp.float32)
    input_grad = input_grad.astype(jnp.bfloat16)
    contract_first = (((0,), (0,)), ((), ()))
    grad_a = lax.dot_general(
        upstream, tokens, contract_first, preferred_element_type=jnp.float32
    )
    grad_b = lax.dot_general(
        hidden, cotangent, contract_first, preferred_element_type=jnp.float32
    )
    outgoing = jnp.stack(
        [
            grad_a.reshape(replicas, owned_rows, columns),
            grad_b.reshape(replicas, owned_rows, columns),
        ],
        1,
    )
    pieces = lax.all_to_all(outgoing, "dp", 0, 0, tiled=True)
    gram = jnp.stack(
        [
            jnp.sum(pieces * pieces[other][None], (2, 3))
            for other in range(replicas)
        ],
        2,
    )
    gram = gram.transpose(1, 0, 2).reshape(1, -1)
    spread = jnp.broadcast_to(gram, (everyone, gram.shape[1]))
    gathered = lax.all_to_all(spread, ("dp", "tensor"), 0, 0, tiled=True)
    gram = jnp.sum(gathered, 0).reshape(2, replicas, replicas)
    weights = tree_weights(gram, levels)
    owned_grad = jnp.sum(pieces * weights.T[:, :, None, None], 0)
    row_start = position * owned_rows
    owned_down = lax.dynamic_slice_in_dim(lowrank_down_factor, row_start, owned_rows, 0)
    owned_up = lax.dynamic_slice_in_dim(lowrank_up_factor, row_start, owned_rows, 0)
    moment_one = 0.9 * first_moment_estimate + 0.1 * owned_grad
    moment_two = 0.95 * second_moment_estimate + 0.05 * owned_grad * owned_grad
    optimizer_update = 0.001 * moment_one / (jnp.sqrt(moment_two) + 1e-08)
    updated_down_factor = owned_down - optimizer_update[0]
    updated_up_factor = owned_up - optimizer_update[1]
    return (input_grad, updated_down_factor, updated_up_factor, moment_one, moment_two)


def solution(mesh):
    placed = (
        P("dp", "tensor"),
        P("dp", "tensor"),
        P(None, "tensor"),
        P(None, "tensor"),
        P(None, "dp", "tensor"),
        P(None, "dp", "tensor"),
    )
    return jax.shard_map(
        body,
        mesh=mesh,
        in_specs=placed,
        out_specs=(
            P("dp", "tensor"),
            P("dp", "tensor"),
            P("dp", "tensor"),
            P(None, "dp", "tensor"),
            P(None, "dp", "tensor"),
        ),
        check_vma=False,
    )
```

```python
import functools

import jax
import jax.numpy as jnp
from jax import lax
from jax.experimental import pallas as pl
from jax.experimental.pallas import tpu as pltpu
from jax.sharding import PartitionSpec as P

SCALE = 2.0
NORM_EPS = 1e-06
LANES = 128
VMEM_LIMIT = 32 * 1024 * 1024
IN_VMEM = pl.BlockSpec(memory_space=pltpu.VMEM)
IN_SMEM = pl.BlockSpec(memory_space=pltpu.SMEM)


def other_of(block, axis, apart):
    route = [(here, here ^ apart) for here in range(lax.axis_size(axis))]
    return lax.ppermute(block, axis, route)


def butterfly_sum(block, axis, apart):
    other = jnp.zeros_like(block)
    while apart < lax.axis_size(axis):
        block = block + other
        other = other_of(block, axis, apart)
        apart *= 2
    return block, other


def exact_dot(left, right, dims):
    return lax.dot_general(
        left,
        right,
        (dims, ((), ())),
        precision=lax.Precision.HIGHEST,
        preferred_element_type=jnp.float32,
    )


def rank_sums(mine_ref, other_ref):
    return (SCALE * (mine_ref[...] + other_ref[...])).astype(jnp.bfloat16)


def gradient(sums, rows_ref):
    return jnp.dot(sums, rows_ref[...], preferred_element_type=jnp.float32)


def rank_block(ref, me, k, owned):
    block = (me ^ k) % (ref.shape[0] // owned)
    return ref[pl.ds(pl.multiple_of(block * owned, owned), owned), :]


def far_kernel(me_ref, mine_ref, other_ref, rows_ref, sums_ref, *refs):
    *piece_refs, grad_ref = refs
    sums = rank_sums(mine_ref, other_ref)
    sums_ref[...] = sums
    grad_ref[...] = gradient(sums, rows_ref)
    owned = piece_refs[0].shape[0]
    for k, piece_ref in enumerate(piece_refs):
        piece_ref[...] = rank_block(grad_ref, me_ref[0], k, owned)


def near_kernel(me_ref, mine_ref, other_ref, tokens_ref, cotangent_ref, sums_ref, *refs):
    *piece_refs, grad_a_ref, grad_b_ref = refs
    sums = rank_sums(mine_ref, other_ref)
    half = sums.shape[0] // 2
    sums_ref[...] = sums[:half]
    grad_a_ref[...] = gradient(sums[:half], tokens_ref)
    grad_b_ref[...] = gradient(sums[half:], cotangent_ref)
    owned = piece_refs[0].shape[0] // 2
    for k, piece_ref in enumerate(piece_refs):
        piece_ref[:owned] = rank_block(grad_a_ref, me_ref[0], k, owned)
        piece_ref[owned:] = rank_block(grad_b_ref, me_ref[0], k, owned)


def pieces_of(factor, refs, replicas, owned):
    near = refs[: replicas // 2]
    far = refs[replicas // 2 : replicas]
    return [ref.at[factor * owned : (factor + 1) * owned] for ref in near] + list(far)


def inner_products(pieces, rows_ref, first):
    replicas = len(pieces)
    columns = pieces[0].shape[1]
    pairs = [(i, j) for i in range(replicas) for j in range(i, replicas)]
    sums = {}
    for start in range(0, columns, LANES):
        parts = [ref[:, start : start + LANES] for ref in pieces]
        for i, j in pairs:
            product = parts[i] * parts[j]
            sums[i, j] = sums[i, j] + product if start else product
    for i, j in pairs:
        row = jnp.sum(sums[i, j], axis=0, keepdims=True)
        at = first + i * replicas + j
        rows_ref[at : at + 1, :] = row
        if i != j:
            at = first + j * replicas + i
            rows_ref[at : at + 1, :] = row


def relabelled(gram, me, replicas):
    lanes = gram.shape[1]
    source = lax.broadcasted_iota(jnp.int32, (lanes, lanes), 0)
    target = lax.broadcasted_iota(jnp.int32, (lanes, lanes), 1)
    chosen = jnp.where(target == source ^ (me * replicas + me), 1.0, 0.0)
    return exact_dot(gram, chosen.astype(jnp.float32), ((1,), (0,)))


def first_gram_kernel(*refs):
    replicas = len(refs) - 1
    owned = refs[replicas - 1].shape[0]
    inner_products(pieces_of(0, refs, replicas, owned), refs[-1], 0)


def second_gram_kernel(me_ref, other_rows_ref, *refs):
    replicas = len(refs) - 2
    owned = refs[replicas - 1].shape[0]
    spread_ref, rows_ref = refs[-2:]
    size = replicas * replicas
    rows_ref[:size, :] = other_rows_ref[...]
    inner_products(pieces_of(1, refs, replicas, owned), rows_ref, size)
    ones = jnp.ones((8, LANES), jnp.float32)
    gram = exact_dot(ones, rows_ref[...], ((1,), (1,)))
    gram = relabelled(gram, me_ref[0], replicas)
    spread_ref[...] = jnp.broadcast_to(gram[:1, :][None], spread_ref.shape)


def tree_weights(gram, replicas):
    size = replicas * replicas
    lanes = gram.shape[1]
    source = lax.broadcasted_iota(jnp.int32, (lanes, lanes), 0)
    target = lax.broadcasted_iota(jnp.int32, (lanes, lanes), 1)
    same_factor = source // size == target // size
    source_i = source % size // replicas
    source_j = source % replicas
    target_i = target % size // replicas
    target_j = target % replicas

    def gather(values, wanted):
        chosen = jnp.where(same_factor & wanted, 1.0, 0.0).astype(jnp.float32)
        return exact_dot(values, chosen, ((1,), (0,)))

    weights = jnp.ones_like(gram)
    level = 0
    while 1 << level < replicas:
        left, right = source_i >> level, source_j >> level
        kept = []
        for target_at in (target_i >> level, target_j >> level):
            norm = gather(gram, (left == target_at) & (right == target_at))
            cross = gather(gram, (left == target_at) & (right == (target_at ^ 1)))
            kept.append(1.0 - cross / (2.0 * (norm + NORM_EPS)))
        gram = gram * kept[0] * kept[1]
        weights = weights * kept[0]
        level += 1
    return weights


def finish_kernel(me_ref, gathered_ref, *refs, replicas):
    half = replicas // 2
    near, far_a, far_b = refs[:half], refs[half : 2 * half], refs[2 * half : 3 * half]
    first_ref, second_ref, down_ref, up_ref = refs[3 * half : 3 * half + 4]
    new_down_ref, new_up_ref, new_first_ref, new_second_ref = refs[3 * half + 4 :]
    gram = jnp.sum(gathered_ref[...], axis=0)
    gram = jnp.broadcast_to(gram, (8, gram.shape[1]))
    weights = tree_weights(relabelled(gram, me_ref[0], replicas), replicas)
    factors = ((far_a, down_ref, new_down_ref), (far_b, up_ref, new_up_ref))
    for factor, (far, old_ref, new_ref) in enumerate(factors):
        owned = old_ref.shape[0]
        combined = jnp.zeros(old_ref.shape, jnp.float32)
        for i, piece_ref in enumerate(pieces_of(factor, near + far, replicas, owned)):
            lane = (factor * replicas + i) * replicas
            combined += weights[:1, lane : lane + 1] * piece_ref[...]
        moment_one = 0.9 * first_ref[factor] + 0.1 * combined
        moment_two = 0.95 * second_ref[factor] + 0.05 * combined * combined
        new_first_ref[factor] = moment_one
        new_second_ref[factor] = moment_two
        change = 0.001 * moment_one / (jnp.sqrt(moment_two) + 1e-08)
        new_ref[...] = old_ref[...] - change


def body(
    tokens,
    cotangent,
    lowrank_down_factor,
    lowrank_up_factor,
    first_moment_estimate,
    second_moment_estimate,
):
    replicas = lax.axis_size("dp")
    everyone = replicas * lax.axis_size("tensor")
    half = replicas // 2
    rows, columns = tokens.shape
    rank = lowrank_down_factor.shape[0]
    owned_rows = first_moment_estimate.shape[1]
    size = replicas * replicas
    me = lax.axis_index("dp")
    position = me.astype(jnp.int32).reshape(1)
    params = pltpu.CompilerParams(vmem_limit_bytes=VMEM_LIMIT)

    def shape(*dims, dtype=jnp.float32):
        return jax.ShapeDtypeStruct(dims, dtype)

    def chip_sum(block, factor):
        partial = lax.dot_general(
            factor,
            block,
            (((1,), (1,)), ((), ())),
            preferred_element_type=jnp.float32,
        )
        return partial + other_of(partial, "tensor", 1)

    def half_of(block, owner):
        start = owner // half * (half * owned_rows)
        return lax.dynamic_slice_in_dim(block, start, half * owned_rows, 0)

    def sent(block, apart):
        route = [(here, here ^ apart) for here in range(replicas)]
        return lax.ppermute(block, "dp", route)

    def far_exchange(sums, block, name):
        sums, *pieces = pl.pallas_call(
            far_kernel,
            in_specs=[IN_SMEM] + [IN_VMEM] * 3,
            out_shape=[shape(rank // 2, rows, dtype=jnp.bfloat16)]
            + [shape(owned_rows, columns)] * half,
            scratch_shapes=[pltpu.VMEM((rank // 2, columns), jnp.float32)],
            compiler_params=params,
            name=name,
        )(position, *sums, block)
        return sums, pieces

    adapter_in = lowrank_down_factor.astype(jnp.bfloat16)
    adapter_out = lowrank_up_factor.astype(jnp.bfloat16)
    upstream = chip_sum(cotangent, adapter_out)
    hidden = chip_sum(tokens, adapter_in)
    far_owner = (me + half) % replicas
    upstream_far = butterfly_sum(half_of(upstream, far_owner), "tensor", 2)
    hidden_far = butterfly_sum(half_of(hidden, far_owner), "tensor", 2)
    near = jnp.concatenate([half_of(upstream, me), half_of(hidden, me)])
    upstream_far, far_a = far_exchange(upstream_far, tokens, "far_a")
    _, far_b = far_exchange(hidden_far, cotangent, "far_b")
    near, far_b = lax.optimization_barrier((near, far_b))
    near = butterfly_sum(near, "tensor", 2)
    far_a = [sent(piece, half + k) for k, piece in enumerate(far_a)]
    far_b = [sent(piece, half + k) for k, piece in enumerate(far_b)]
    upstream_near, own, *near = pl.pallas_call(
        near_kernel,
        in_specs=[IN_SMEM] + [IN_VMEM] * 4,
        out_shape=[shape(rank // 2, rows, dtype=jnp.bfloat16)]
        + [shape(2 * owned_rows, columns)] * half,
        scratch_shapes=[pltpu.VMEM((rank // 2, columns), jnp.float32)] * 2,
        compiler_params=params,
        name="near",
    )(position, *near, tokens, cotangent)
    near = [own] + [sent(piece, k + 1) for k, piece in enumerate(near)]

    upstream = jnp.where(
        me < half,
        jnp.concatenate([upstream_near, upstream_far]),
        jnp.concatenate([upstream_far, upstream_near]),
    )
    input_grad = lax.dot_general(
        upstream,
        adapter_in,
        (((0,), (0,)), ((), ())),
        preferred_element_type=jnp.float32,
    )
    input_grad = input_grad.astype(jnp.bfloat16)
    owned_down = lax.dynamic_slice_in_dim(
        lowrank_down_factor, me * owned_rows, owned_rows, 0
    )
    owned_up = lax.dynamic_slice_in_dim(
        lowrank_up_factor, me * owned_rows, owned_rows, 0
    )
    near, input_grad, owned_down, owned_up = lax.optimization_barrier(
        (near, input_grad, owned_down, owned_up)
    )

    rows_a = pl.pallas_call(
        first_gram_kernel,
        out_shape=shape(size, LANES),
        compiler_params=params,
        name="gram_a",
    )(*near, *far_a)
    spread = pl.pallas_call(
        second_gram_kernel,
        in_specs=[IN_SMEM] + [IN_VMEM] * (1 + replicas),
        out_shape=shape(everyone, 1, 2 * size),
        scratch_shapes=[pltpu.VMEM((2 * size, LANES), jnp.float32)],
        compiler_params=params,
        name="gram_b",
    )(position, rows_a, *near, *far_b)
    gathered = lax.all_to_all(spread, ("dp", "tensor"), 0, 0, tiled=True)

    row_out = shape(owned_rows, columns)
    moment_out = shape(*first_moment_estimate.shape)
    updated_down_factor, updated_up_factor, moment_one, moment_two = pl.pallas_call(
        functools.partial(finish_kernel, replicas=replicas),
        in_specs=[IN_SMEM] + [IN_VMEM] * (3 * half + 5),
        out_shape=(row_out, row_out, moment_out, moment_out),
        compiler_params=params,
        name="finish",
    )(
        position,
        gathered,
        *near,
        *far_a,
        *far_b,
        first_moment_estimate,
        second_moment_estimate,
        owned_down,
        owned_up,
    )
    return (input_grad, updated_down_factor, updated_up_factor, moment_one, moment_two)


def solution(mesh):
    placed = (
        P("dp", "tensor"),
        P("dp", "tensor"),
        P(None, "tensor"),
        P(None, "tensor"),
        P(None, "dp", "tensor"),
        P(None, "dp", "tensor"),
    )
    return jax.shard_map(
        body,
        mesh=mesh,
        in_specs=placed,
        out_specs=(
            P("dp", "tensor"),
            P("dp", "tensor"),
            P("dp", "tensor"),
            P(None, "dp", "tensor"),
            P(None, "dp", "tensor"),
        ),
        check_vma=False,
    )
```

```python
import functools

import jax
import jax.numpy as jnp
from jax import lax
from jax.experimental import pallas as pl
from jax.experimental.pallas import tpu as pltpu
from jax.sharding import PartitionSpec as P

SCALE = 2.0
NORM_EPS = 1e-06
LANES = 128
VMEM_LIMIT = 32 * 1024 * 1024
IN_VMEM = pl.BlockSpec(memory_space=pltpu.VMEM)
IN_SMEM = pl.BlockSpec(memory_space=pltpu.SMEM)


def other_of(block, axis, apart):
    route = [(here, here ^ apart) for here in range(lax.axis_size(axis))]
    return lax.ppermute(block, axis, route)


def butterfly_sum(block, axis, apart):
    other = jnp.zeros_like(block)
    while apart < lax.axis_size(axis):
        block = block + other
        other = other_of(block, axis, apart)
        apart *= 2
    return block, other


def exact_dot(left, right, dims):
    return lax.dot_general(
        left,
        right,
        (dims, ((), ())),
        precision=lax.Precision.HIGHEST,
        preferred_element_type=jnp.float32,
    )


def pieces_of(factor, refs, replicas, owned):
    near = refs[: replicas // 2]
    far = refs[replicas // 2 : replicas]
    return [ref.at[factor * owned : (factor + 1) * owned] for ref in near] + list(far)


def inner_products(pieces, rows_ref, first):
    replicas = len(pieces)
    columns = pieces[0].shape[1]
    pairs = [(i, j) for i in range(replicas) for j in range(i, replicas)]
    sums = {}
    for start in range(0, columns, LANES):
        parts = [ref[:, start : start + LANES] for ref in pieces]
        for i, j in pairs:
            product = parts[i] * parts[j]
            sums[i, j] = sums[i, j] + product if start else product
    for i, j in pairs:
        row = jnp.sum(sums[i, j], axis=0, keepdims=True)
        at = first + i * replicas + j
        rows_ref[at : at + 1, :] = row
        if i != j:
            at = first + j * replicas + i
            rows_ref[at : at + 1, :] = row


def relabelled(gram, me, replicas):
    lanes = gram.shape[1]
    source = lax.broadcasted_iota(jnp.int32, (lanes, lanes), 0)
    target = lax.broadcasted_iota(jnp.int32, (lanes, lanes), 1)
    chosen = jnp.where(target == source ^ (me * replicas + me), 1.0, 0.0)
    return exact_dot(gram, chosen.astype(jnp.float32), ((1,), (0,)))


def first_gram_kernel(*refs):
    replicas = len(refs) - 1
    owned = refs[replicas - 1].shape[0]
    inner_products(pieces_of(0, refs, replicas, owned), refs[-1], 0)


def second_gram_kernel(me_ref, other_rows_ref, *refs):
    replicas = len(refs) - 2
    owned = refs[replicas - 1].shape[0]
    spread_ref, rows_ref = refs[-2:]
    size = replicas * replicas
    rows_ref[:size, :] = other_rows_ref[...]
    inner_products(pieces_of(1, refs, replicas, owned), rows_ref, size)
    ones = jnp.ones((8, LANES), jnp.float32)
    gram = exact_dot(ones, rows_ref[...], ((1,), (1,)))
    gram = relabelled(gram, me_ref[0], replicas)
    spread_ref[...] = jnp.broadcast_to(gram[:1, :][None], spread_ref.shape)


def tree_weights(gram, replicas):
    size = replicas * replicas
    lanes = gram.shape[1]
    source = lax.broadcasted_iota(jnp.int32, (lanes, lanes), 0)
    target = lax.broadcasted_iota(jnp.int32, (lanes, lanes), 1)
    same_factor = source // size == target // size
    source_i = source % size // replicas
    source_j = source % replicas
    target_i = target % size // replicas
    target_j = target % replicas

    def gather(values, wanted):
        chosen = jnp.where(same_factor & wanted, 1.0, 0.0).astype(jnp.float32)
        return exact_dot(values, chosen, ((1,), (0,)))

    weights = jnp.ones_like(gram)
    level = 0
    while 1 << level < replicas:
        left, right = source_i >> level, source_j >> level
        kept = []
        for target_at in (target_i >> level, target_j >> level):
            norm = gather(gram, (left == target_at) & (right == target_at))
            cross = gather(gram, (left == target_at) & (right == (target_at ^ 1)))
            kept.append(1.0 - cross / (2.0 * (norm + NORM_EPS)))
        gram = gram * kept[0] * kept[1]
        weights = weights * kept[0]
        level += 1
    return weights


def finish_kernel(me_ref, gathered_ref, *refs, replicas):
    half = replicas // 2
    near, far_a, far_b = refs[:half], refs[half : 2 * half], refs[2 * half : 3 * half]
    first_ref, second_ref, down_ref, up_ref = refs[3 * half : 3 * half + 4]
    new_down_ref, new_up_ref, new_first_ref, new_second_ref = refs[3 * half + 4 :]
    gram = jnp.sum(gathered_ref[...], axis=0)
    gram = jnp.broadcast_to(gram, (8, gram.shape[1]))
    weights = tree_weights(relabelled(gram, me_ref[0], replicas), replicas)
    factors = ((far_a, down_ref, new_down_ref), (far_b, up_ref, new_up_ref))
    for factor, (far, old_ref, new_ref) in enumerate(factors):
        owned = old_ref.shape[0]
        combined = jnp.zeros(old_ref.shape, jnp.float32)
        for i, piece_ref in enumerate(pieces_of(factor, near + far, replicas, owned)):
            lane = (factor * replicas + i) * replicas
            combined += weights[:1, lane : lane + 1] * piece_ref[...]
        moment_one = 0.9 * first_ref[factor] + 0.1 * combined
        moment_two = 0.95 * second_ref[factor] + 0.05 * combined * combined
        new_first_ref[factor] = moment_one
        new_second_ref[factor] = moment_two
        change = 0.001 * moment_one / (jnp.sqrt(moment_two) + 1e-08)
        new_ref[...] = old_ref[...] - change


def body(
    tokens,
    cotangent,
    lowrank_down_factor,
    lowrank_up_factor,
    first_moment_estimate,
    second_moment_estimate,
):
    replicas = lax.axis_size("dp")
    everyone = replicas * lax.axis_size("tensor")
    half = replicas // 2
    rows, columns = tokens.shape
    rank = lowrank_down_factor.shape[0]
    owned_rows = first_moment_estimate.shape[1]
    size = replicas * replicas
    me = lax.axis_index("dp")
    position = me.astype(jnp.int32).reshape(1)
    params = pltpu.CompilerParams(vmem_limit_bytes=VMEM_LIMIT)

    def shape(*dims, dtype=jnp.float32):
        return jax.ShapeDtypeStruct(dims, dtype)

    def projected(block, factor):
        return lax.dot_general(
            factor,
            block,
            (((1,), (1,)), ((), ())),
            preferred_element_type=jnp.float32,
        )

    def half_of(block, owner):
        start = owner // half * (half * owned_rows)
        return lax.dynamic_slice_in_dim(block, start, half * owned_rows, 0)

    def sent(block, apart):
        route = [(here, here ^ apart) for here in range(replicas)]
        return lax.ppermute(block, "dp", route)

    def rank_sums(addends):
        return (SCALE * (addends[0] + addends[1])).astype(jnp.bfloat16)

    def gradient(sums, block):
        return jnp.dot(sums, block, preferred_element_type=jnp.float32)

    def pieces_for(grad):
        return [
            lax.dynamic_slice_in_dim(
                grad, (me ^ k) % half * owned_rows, owned_rows, 0
            )
            for k in range(half)
        ]

    adapter_in = lowrank_down_factor.astype(jnp.bfloat16)
    adapter_out = lowrank_up_factor.astype(jnp.bfloat16)
    upstream = projected(cotangent, adapter_out)
    hidden = projected(tokens, adapter_in)
    upstream = upstream + other_of(upstream, "tensor", 1)
    hidden = hidden + other_of(hidden, "tensor", 1)
    far_owner = (me + half) % replicas
    upstream_far = rank_sums(butterfly_sum(half_of(upstream, far_owner), "tensor", 2))
    far_a = pieces_for(gradient(upstream_far, tokens))
    rest = jnp.concatenate(
        [half_of(hidden, far_owner), half_of(hidden, me), half_of(upstream, me)]
    )
    rest, upstream_far, far_a = lax.optimization_barrier((rest, upstream_far, far_a))
    far_a = [sent(piece, half + k) for k, piece in enumerate(far_a)]
    rest = rank_sums(butterfly_sum(rest, "tensor", 2))
    hidden, upstream_near = rest[:rank], rest[rank:]
    grad_b = gradient(hidden, cotangent)
    far_b = pieces_for(grad_b[: rank // 2])
    near_b = pieces_for(grad_b[rank // 2 :])
    near_a = pieces_for(gradient(upstream_near, tokens))
    near = [jnp.concatenate(pair) for pair in zip(near_a, near_b)]
    far_b = [sent(piece, half + k) for k, piece in enumerate(far_b)]
    near = near[:1] + [sent(piece, k) for k, piece in enumerate(near) if k]

    upstream = jnp.where(
        me < half,
        jnp.concatenate([upstream_near, upstream_far]),
        jnp.concatenate([upstream_far, upstream_near]),
    )
    input_grad = lax.dot_general(
        upstream,
        adapter_in,
        (((0,), (0,)), ((), ())),
        preferred_element_type=jnp.float32,
    )
    input_grad = input_grad.astype(jnp.bfloat16)
    owned_down = lax.dynamic_slice_in_dim(
        lowrank_down_factor, me * owned_rows, owned_rows, 0
    )
    owned_up = lax.dynamic_slice_in_dim(
        lowrank_up_factor, me * owned_rows, owned_rows, 0
    )
    near, input_grad, owned_down, owned_up = lax.optimization_barrier(
        (near, input_grad, owned_down, owned_up)
    )

    rows_a = pl.pallas_call(
        first_gram_kernel,
        out_shape=shape(size, LANES),
        compiler_params=params,
        name="gram_a",
    )(*near, *far_a)
    spread = pl.pallas_call(
        second_gram_kernel,
        in_specs=[IN_SMEM] + [IN_VMEM] * (1 + replicas),
        out_shape=shape(everyone, 1, 2 * size),
        scratch_shapes=[pltpu.VMEM((2 * size, LANES), jnp.float32)],
        compiler_params=params,
        name="gram_b",
    )(position, rows_a, *near, *far_b)
    gathered = lax.all_to_all(spread, ("dp", "tensor"), 0, 0, tiled=True)

    row_out = shape(owned_rows, columns)
    moment_out = shape(*first_moment_estimate.shape)
    updated_down_factor, updated_up_factor, moment_one, moment_two = pl.pallas_call(
        functools.partial(finish_kernel, replicas=replicas),
        in_specs=[IN_SMEM] + [IN_VMEM] * (3 * half + 5),
        out_shape=(row_out, row_out, moment_out, moment_out),
        compiler_params=params,
        name="finish",
    )(
        position,
        gathered,
        *near,
        *far_a,
        *far_b,
        first_moment_estimate,
        second_moment_estimate,
        owned_down,
        owned_up,
    )
    return (input_grad, updated_down_factor, updated_up_factor, moment_one, moment_two)


def solution(mesh):
    placed = (
        P("dp", "tensor"),
        P("dp", "tensor"),
        P(None, "tensor"),
        P(None, "tensor"),
        P(None, "dp", "tensor"),
        P(None, "dp", "tensor"),
    )
    return jax.shard_map(
        body,
        mesh=mesh,
        in_specs=placed,
        out_specs=(
            P("dp", "tensor"),
            P("dp", "tensor"),
            P("dp", "tensor"),
            P(None, "dp", "tensor"),
            P(None, "dp", "tensor"),
        ),
        check_vma=False,
    )
```

```python
import functools

import jax
import jax.numpy as jnp
from jax import lax
from jax.experimental import pallas as pl
from jax.experimental.pallas import tpu as pltpu
from jax.sharding import PartitionSpec as P

SCALE = 2.0
NORM_EPS = 1e-06
LANES = 128
VMEM_LIMIT = 32 * 1024 * 1024
IN_VMEM = pl.BlockSpec(memory_space=pltpu.VMEM)
IN_SMEM = pl.BlockSpec(memory_space=pltpu.SMEM)


def other_of(block, axis, apart):
    route = [(here, here ^ apart) for here in range(lax.axis_size(axis))]
    return lax.ppermute(block, axis, route)


def butterfly_sum(block, axis, apart):
    other = jnp.zeros_like(block)
    while apart < lax.axis_size(axis):
        block = block + other
        other = other_of(block, axis, apart)
        apart *= 2
    return block, other


def exact_dot(left, right, dims):
    return lax.dot_general(
        left,
        right,
        (dims, ((), ())),
        precision=lax.Precision.HIGHEST,
        preferred_element_type=jnp.float32,
    )


def pieces_of(factor, refs, replicas, owned):
    near = refs[: replicas // 2]
    far = refs[replicas // 2 : replicas]
    return [ref.at[factor * owned : (factor + 1) * owned] for ref in near] + list(far)


def inner_products(pieces, rows_ref, first):
    replicas = len(pieces)
    columns = pieces[0].shape[1]
    pairs = [(i, j) for i in range(replicas) for j in range(i, replicas)]
    sums = {}
    for start in range(0, columns, LANES):
        parts = [ref[:, start : start + LANES] for ref in pieces]
        for i, j in pairs:
            product = parts[i] * parts[j]
            sums[i, j] = sums[i, j] + product if start else product
    for i, j in pairs:
        row = jnp.sum(sums[i, j], axis=0, keepdims=True)
        at = first + i * replicas + j
        rows_ref[at : at + 1, :] = row
        if i != j:
            at = first + j * replicas + i
            rows_ref[at : at + 1, :] = row


def relabelled(gram, me, replicas):
    lanes = gram.shape[1]
    source = lax.broadcasted_iota(jnp.int32, (lanes, lanes), 0)
    target = lax.broadcasted_iota(jnp.int32, (lanes, lanes), 1)
    chosen = jnp.where(target == source ^ (me * replicas + me), 1.0, 0.0)
    return exact_dot(gram, chosen.astype(jnp.float32), ((1,), (0,)))


def first_gram_kernel(*refs):
    replicas = len(refs) - 1
    owned = refs[replicas - 1].shape[0]
    inner_products(pieces_of(0, refs, replicas, owned), refs[-1], 0)


def second_gram_kernel(me_ref, other_rows_ref, *refs):
    replicas = len(refs) - 2
    owned = refs[replicas - 1].shape[0]
    spread_ref, rows_ref = refs[-2:]
    size = replicas * replicas
    rows_ref[:size, :] = other_rows_ref[...]
    inner_products(pieces_of(1, refs, replicas, owned), rows_ref, size)
    ones = jnp.ones((8, LANES), jnp.float32)
    gram = exact_dot(ones, rows_ref[...], ((1,), (1,)))
    gram = relabelled(gram, me_ref[0], replicas)
    spread_ref[...] = jnp.broadcast_to(gram[:1, :][None], spread_ref.shape)


def tree_weights(gram, replicas):
    size = replicas * replicas
    lanes = gram.shape[1]
    source = lax.broadcasted_iota(jnp.int32, (lanes, lanes), 0)
    target = lax.broadcasted_iota(jnp.int32, (lanes, lanes), 1)
    same_factor = source // size == target // size
    source_i = source % size // replicas
    source_j = source % replicas
    target_i = target % size // replicas
    target_j = target % replicas

    def gather(values, wanted):
        chosen = jnp.where(same_factor & wanted, 1.0, 0.0).astype(jnp.float32)
        return exact_dot(values, chosen, ((1,), (0,)))

    weights = jnp.ones_like(gram)
    level = 0
    while 1 << level < replicas:
        left, right = source_i >> level, source_j >> level
        kept = []
        for target_at in (target_i >> level, target_j >> level):
            norm = gather(gram, (left == target_at) & (right == target_at))
            cross = gather(gram, (left == target_at) & (right == (target_at ^ 1)))
            kept.append(1.0 - cross / (2.0 * (norm + NORM_EPS)))
        gram = gram * kept[0] * kept[1]
        weights = weights * kept[0]
        level += 1
    return weights


def finish_kernel(me_ref, gathered_ref, *refs, replicas):
    half = replicas // 2
    near, far_a, far_b = refs[:half], refs[half : 2 * half], refs[2 * half : 3 * half]
    first_ref, second_ref, down_ref, up_ref = refs[3 * half : 3 * half + 4]
    new_down_ref, new_up_ref, new_first_ref, new_second_ref = refs[3 * half + 4 :]
    gram = jnp.sum(gathered_ref[...], axis=0)
    gram = jnp.broadcast_to(gram, (8, gram.shape[1]))
    weights = tree_weights(relabelled(gram, me_ref[0], replicas), replicas)
    factors = ((far_a, down_ref, new_down_ref), (far_b, up_ref, new_up_ref))
    for factor, (far, old_ref, new_ref) in enumerate(factors):
        owned = old_ref.shape[0]
        combined = jnp.zeros(old_ref.shape, jnp.float32)
        for i, piece_ref in enumerate(pieces_of(factor, near + far, replicas, owned)):
            lane = (factor * replicas + i) * replicas
            combined += weights[:1, lane : lane + 1] * piece_ref[...]
        moment_one = 0.9 * first_ref[factor] + 0.1 * combined
        moment_two = 0.95 * second_ref[factor] + 0.05 * combined * combined
        new_first_ref[factor] = moment_one
        new_second_ref[factor] = moment_two
        change = 0.001 * moment_one / (jnp.sqrt(moment_two) + 1e-08)
        new_ref[...] = old_ref[...] - change


def body(
    tokens,
    cotangent,
    lowrank_down_factor,
    lowrank_up_factor,
    first_moment_estimate,
    second_moment_estimate,
):
    replicas = lax.axis_size("dp")
    everyone = replicas * lax.axis_size("tensor")
    half = replicas // 2
    rows, columns = tokens.shape
    rank = lowrank_down_factor.shape[0]
    owned_rows = first_moment_estimate.shape[1]
    size = replicas * replicas
    me = lax.axis_index("dp")
    position = me.astype(jnp.int32).reshape(1)
    params = pltpu.CompilerParams(vmem_limit_bytes=VMEM_LIMIT)

    def shape(*dims, dtype=jnp.float32):
        return jax.ShapeDtypeStruct(dims, dtype)

    def projected(block, factor):
        return lax.dot_general(
            factor,
            block,
            (((1,), (1,)), ((), ())),
            preferred_element_type=jnp.float32,
        )

    def half_of(block, owner):
        start = owner // half * (half * owned_rows)
        return lax.dynamic_slice_in_dim(block, start, half * owned_rows, 0)

    def sent(block, apart):
        route = [(here, here ^ apart) for here in range(replicas)]
        return lax.ppermute(block, "dp", route)

    def rank_sums(addends):
        return (SCALE * (addends[0] + addends[1])).astype(jnp.bfloat16)

    def gradient(sums, block):
        return jnp.dot(sums, block, preferred_element_type=jnp.float32)

    def pieces_for(grad):
        return [
            lax.dynamic_slice_in_dim(
                grad, (me ^ k) % half * owned_rows, owned_rows, 0
            )
            for k in range(half)
        ]

    adapter_in = lowrank_down_factor.astype(jnp.bfloat16)
    adapter_out = lowrank_up_factor.astype(jnp.bfloat16)
    adapter_in = lax.optimization_barrier(adapter_in)
    upstream = projected(cotangent, adapter_out)
    hidden = projected(tokens, adapter_in)
    upstream = upstream + other_of(upstream, "tensor", 1)
    hidden = hidden + other_of(hidden, "tensor", 1)
    far_owner = (me + half) % replicas
    upstream_far = rank_sums(butterfly_sum(half_of(upstream, far_owner), "tensor", 2))
    far_a = pieces_for(gradient(upstream_far, tokens))
    rest = jnp.concatenate(
        [half_of(hidden, far_owner), half_of(hidden, me), half_of(upstream, me)]
    )
    rest, upstream_far, far_a = lax.optimization_barrier((rest, upstream_far, far_a))
    far_a = [sent(piece, half + k) for k, piece in enumerate(far_a)]
    rest = rank_sums(butterfly_sum(rest, "tensor", 2))
    hidden, upstream_near = rest[:rank], rest[rank:]
    grad_b = gradient(hidden, cotangent)
    far_b = pieces_for(grad_b[: rank // 2])
    near_b = pieces_for(grad_b[rank // 2 :])
    near_a = pieces_for(gradient(upstream_near, tokens))
    near = [jnp.concatenate(pair) for pair in zip(near_a, near_b)]
    far_b = [sent(piece, half + k) for k, piece in enumerate(far_b)]
    near = near[:1] + [sent(piece, k) for k, piece in enumerate(near) if k]

    upstream = jnp.where(
        me < half,
        jnp.concatenate([upstream_near, upstream_far]),
        jnp.concatenate([upstream_far, upstream_near]),
    )
    input_grad = lax.dot_general(
        upstream,
        adapter_in,
        (((0,), (0,)), ((), ())),
        preferred_element_type=jnp.float32,
    )
    input_grad = input_grad.astype(jnp.bfloat16)
    owned_down = lax.dynamic_slice_in_dim(
        lowrank_down_factor, me * owned_rows, owned_rows, 0
    )
    owned_up = lax.dynamic_slice_in_dim(
        lowrank_up_factor, me * owned_rows, owned_rows, 0
    )
    near, input_grad, owned_down, owned_up = lax.optimization_barrier(
        (near, input_grad, owned_down, owned_up)
    )

    rows_a = pl.pallas_call(
        first_gram_kernel,
        out_shape=shape(size, LANES),
        compiler_params=params,
        name="gram_a",
    )(*near, *far_a)
    spread = pl.pallas_call(
        second_gram_kernel,
        in_specs=[IN_SMEM] + [IN_VMEM] * (1 + replicas),
        out_shape=shape(everyone, 1, 2 * size),
        scratch_shapes=[pltpu.VMEM((2 * size, LANES), jnp.float32)],
        compiler_params=params,
        name="gram_b",
    )(position, rows_a, *near, *far_b)
    gathered = lax.all_to_all(spread, ("dp", "tensor"), 0, 0, tiled=True)

    row_out = shape(owned_rows, columns)
    moment_out = shape(*first_moment_estimate.shape)
    updated_down_factor, updated_up_factor, moment_one, moment_two = pl.pallas_call(
        functools.partial(finish_kernel, replicas=replicas),
        in_specs=[IN_SMEM] + [IN_VMEM] * (3 * half + 5),
        out_shape=(row_out, row_out, moment_out, moment_out),
        compiler_params=params,
        name="finish",
    )(
        position,
        gathered,
        *near,
        *far_a,
        *far_b,
        first_moment_estimate,
        second_moment_estimate,
        owned_down,
        owned_up,
    )
    return (input_grad, updated_down_factor, updated_up_factor, moment_one, moment_two)


def solution(mesh):
    placed = (
        P("dp", "tensor"),
        P("dp", "tensor"),
        P(None, "tensor"),
        P(None, "tensor"),
        P(None, "dp", "tensor"),
        P(None, "dp", "tensor"),
    )
    return jax.shard_map(
        body,
        mesh=mesh,
        in_specs=placed,
        out_specs=(
            P("dp", "tensor"),
            P("dp", "tensor"),
            P("dp", "tensor"),
            P(None, "dp", "tensor"),
            P(None, "dp", "tensor"),
        ),
        check_vma=False,
    )
```

```python
import functools

import jax
import jax.numpy as jnp
from jax import lax
from jax.experimental import pallas as pl
from jax.experimental.pallas import tpu as pltpu
from jax.sharding import PartitionSpec as P

SCALE = 2.0
NORM_EPS = 1e-06
LANES = 128
VMEM_LIMIT = 32 * 1024 * 1024
IN_VMEM = pl.BlockSpec(memory_space=pltpu.VMEM)
IN_SMEM = pl.BlockSpec(memory_space=pltpu.SMEM)


def other_of(block, axis, apart):
    route = [(here, here ^ apart) for here in range(lax.axis_size(axis))]
    return lax.ppermute(block, axis, route)


def butterfly_sum(block, axis, apart):
    other = jnp.zeros_like(block)
    while apart < lax.axis_size(axis):
        block = block + other
        other = other_of(block, axis, apart)
        apart *= 2
    return block, other


def pieces_of(factor, refs, replicas, owned):
    near = refs[: replicas // 2]
    far = refs[replicas // 2 : replicas]
    return [ref.at[factor * owned : (factor + 1) * owned] for ref in near] + list(far)


def inner_products(pieces, rows_ref, first, me):
    replicas = len(pieces)
    columns = pieces[0].shape[1]
    pairs = [(i, j) for i in range(replicas) for j in range(i, replicas)]
    sums = {}
    for start in range(0, columns, LANES):
        parts = [ref[:, start : start + LANES] for ref in pieces]
        for i, j in pairs:
            product = parts[i] * parts[j]
            sums[i, j] = sums[i, j] + product if start else product
    for i, j in pairs:
        row = jnp.sum(sums[i, j], axis=0, keepdims=True)
        one, two = i ^ me, j ^ me
        rows_ref[pl.ds(first + one * replicas + two, 1), :] = row
        if i != j:
            rows_ref[pl.ds(first + two * replicas + one, 1), :] = row


def tree_maps(maps_ref, me, replicas):
    size = replicas * replicas
    lanes = maps_ref.shape[1]
    source = lax.broadcasted_iota(jnp.int32, (lanes, lanes), 0)
    target = lax.broadcasted_iota(jnp.int32, (lanes, lanes), 1)
    for level in range(maps_ref.shape[0]):
        at = source ^ (me * replicas + me) if level == 0 else source
        same_factor = at // size == target // size
        left, right = at % size // replicas >> level, at % replicas >> level
        maps = []
        for group in (target % size // replicas >> level, target % replicas >> level):
            maps.append(same_factor & (left == group) & (right == group))
            maps.append(same_factor & (left == group) & (right == (group ^ 1)))
        maps.append(at == target)
        for place, chosen in enumerate(maps):
            maps_ref[level, :, place * lanes : (place + 1) * lanes] = jnp.where(
                chosen, 1.0, 0.0
            ).astype(maps_ref.dtype)


def mapped(values, map_ref, count):
    high = values.astype(jnp.bfloat16).astype(jnp.float32)
    middle = (values - high).astype(jnp.bfloat16).astype(jnp.float32)
    row = lax.broadcasted_iota(jnp.int32, values.shape, 0)
    parts = jnp.where(row == 0, high, jnp.where(row == 1, middle, values - high - middle))
    parts = jnp.where(row < 3, parts, 0.0).astype(jnp.bfloat16)
    lanes = values.shape[1]
    found = jnp.dot(
        parts, map_ref[:, : count * lanes], preferred_element_type=jnp.float32
    )
    found = jnp.broadcast_to(jnp.sum(found, axis=0, keepdims=True), found.shape)
    return [found[:, k * lanes : (k + 1) * lanes] for k in range(count)]


def tree_weights(gram, maps_ref):
    weights = jnp.ones_like(gram)
    for level in range(maps_ref.shape[0]):
        if level == 0:
            *terms, gram = mapped(gram, maps_ref.at[level], 5)
        else:
            terms = mapped(gram, maps_ref.at[level], 4)
        kept = []
        for norm, cross in (terms[:2], terms[2:]):
            norm = jnp.maximum(norm, 0.0)
            kept.append(1.0 - cross / (2.0 * (norm + NORM_EPS)))
        gram = gram * kept[0] * kept[1]
        weights = weights * kept[0]
    return weights


def first_gram_kernel(me_ref, *refs):
    *piece_refs, rows_ref, maps_ref = refs
    replicas = len(piece_refs)
    owned = piece_refs[-1].shape[0]
    inner_products(pieces_of(0, piece_refs, replicas, owned), rows_ref, 0, me_ref[0])
    tree_maps(maps_ref, me_ref[0], replicas)


def second_gram_kernel(me_ref, other_rows_ref, *refs):
    *piece_refs, spread_ref, rows_ref = refs
    replicas = len(piece_refs)
    owned = piece_refs[-1].shape[0]
    size = replicas * replicas
    rows_ref[:size, :] = other_rows_ref[...]
    inner_products(pieces_of(1, piece_refs, replicas, owned), rows_ref, size, me_ref[0])
    gram = jnp.sum(rows_ref[...].T, axis=0, keepdims=True)
    spread_ref[...] = jnp.broadcast_to(gram[None], spread_ref.shape)


def finish_kernel(gathered_ref, maps_ref, *refs, replicas):
    half = replicas // 2
    near, far_a, far_b = refs[:half], refs[half : 2 * half], refs[2 * half : 3 * half]
    first_ref, second_ref, down_ref, up_ref = refs[3 * half : 3 * half + 4]
    new_down_ref, new_up_ref, new_first_ref, new_second_ref = refs[3 * half + 4 :]
    gram = jnp.sum(gathered_ref[...], axis=0)
    gram = jnp.broadcast_to(gram, (16, gram.shape[1]))
    weights = tree_weights(gram, maps_ref)
    factors = ((far_a, down_ref, new_down_ref), (far_b, up_ref, new_up_ref))
    for factor, (far, old_ref, new_ref) in enumerate(factors):
        owned = old_ref.shape[0]
        combined = jnp.zeros(old_ref.shape, jnp.float32)
        for i, piece_ref in enumerate(pieces_of(factor, near + far, replicas, owned)):
            lane = (factor * replicas + i) * replicas
            combined += weights[:1, lane : lane + 1] * piece_ref[...]
        moment_one = 0.9 * first_ref[factor] + 0.1 * combined
        moment_two = 0.95 * second_ref[factor] + 0.05 * combined * combined
        new_first_ref[factor] = moment_one
        new_second_ref[factor] = moment_two
        change = 0.001 * moment_one / (jnp.sqrt(moment_two) + 1e-08)
        new_ref[...] = old_ref[...] - change


def body(
    tokens,
    cotangent,
    lowrank_down_factor,
    lowrank_up_factor,
    first_moment_estimate,
    second_moment_estimate,
):
    replicas = lax.axis_size("dp")
    everyone = replicas * lax.axis_size("tensor")
    half = replicas // 2
    rows, columns = tokens.shape
    rank = lowrank_down_factor.shape[0]
    owned_rows = first_moment_estimate.shape[1]
    size = replicas * replicas
    levels = replicas.bit_length() - 1
    me = lax.axis_index("dp")
    position = me.astype(jnp.int32).reshape(1)
    params = pltpu.CompilerParams(vmem_limit_bytes=VMEM_LIMIT)

    def shape(*dims, dtype=jnp.float32):
        return jax.ShapeDtypeStruct(dims, dtype)

    def projected(block, factor):
        return lax.dot_general(
            factor,
            block,
            (((1,), (1,)), ((), ())),
            preferred_element_type=jnp.float32,
        )

    def half_of(block, owner):
        start = owner // half * (half * owned_rows)
        return lax.dynamic_slice_in_dim(block, start, half * owned_rows, 0)

    def sent(block, apart):
        route = [(here, here ^ apart) for here in range(replicas)]
        return lax.ppermute(block, "dp", route)

    def rank_sums(addends):
        return (SCALE * (addends[0] + addends[1])).astype(jnp.bfloat16)

    def gradient(sums, block):
        return jnp.dot(sums, block, preferred_element_type=jnp.float32)

    def pieces_for(grad):
        return [
            lax.dynamic_slice_in_dim(
                grad, (me ^ k) % half * owned_rows, owned_rows, 0
            )
            for k in range(half)
        ]

    adapter_in = lowrank_down_factor.astype(jnp.bfloat16)
    adapter_out = lowrank_up_factor.astype(jnp.bfloat16)
    adapter_in = lax.optimization_barrier(adapter_in)
    upstream = projected(cotangent, adapter_out)
    hidden = projected(tokens, adapter_in)
    upstream = upstream + other_of(upstream, "tensor", 1)
    hidden = hidden + other_of(hidden, "tensor", 1)
    far_owner = (me + half) % replicas
    upstream_far = rank_sums(butterfly_sum(half_of(upstream, far_owner), "tensor", 2))
    far_a = pieces_for(gradient(upstream_far, tokens))
    rest = jnp.concatenate(
        [half_of(hidden, far_owner), half_of(hidden, me), half_of(upstream, me)]
    )
    rest, upstream_far, far_a = lax.optimization_barrier((rest, upstream_far, far_a))
    far_a = [sent(piece, half + k) for k, piece in enumerate(far_a)]
    rest = rank_sums(butterfly_sum(rest, "tensor", 2))
    hidden, upstream_near = rest[:rank], rest[rank:]
    grad_b = gradient(hidden, cotangent)
    far_b = pieces_for(grad_b[: rank // 2])
    near_b = pieces_for(grad_b[rank // 2 :])
    near_a = pieces_for(gradient(upstream_near, tokens))
    near = [jnp.concatenate(pair) for pair in zip(near_a, near_b)]
    far_b = [sent(piece, half + k) for k, piece in enumerate(far_b)]
    near = near[:1] + [sent(piece, k) for k, piece in enumerate(near) if k]

    upstream = jnp.where(
        me < half,
        jnp.concatenate([upstream_near, upstream_far]),
        jnp.concatenate([upstream_far, upstream_near]),
    )
    input_grad = lax.dot_general(
        upstream,
        adapter_in,
        (((0,), (0,)), ((), ())),
        preferred_element_type=jnp.float32,
    )
    input_grad = input_grad.astype(jnp.bfloat16)
    owned_down = lax.dynamic_slice_in_dim(
        lowrank_down_factor, me * owned_rows, owned_rows, 0
    )
    owned_up = lax.dynamic_slice_in_dim(
        lowrank_up_factor, me * owned_rows, owned_rows, 0
    )
    near, input_grad, owned_down, owned_up = lax.optimization_barrier(
        (near, input_grad, owned_down, owned_up)
    )

    rows_a, maps = pl.pallas_call(
        first_gram_kernel,
        in_specs=[IN_SMEM] + [IN_VMEM] * replicas,
        out_shape=[
            shape(size, LANES),
            shape(levels, 2 * size, 10 * size, dtype=jnp.bfloat16),
        ],
        compiler_params=params,
        name="gram_a",
    )(position, *near, *far_a)
    spread = pl.pallas_call(
        second_gram_kernel,
        in_specs=[IN_SMEM] + [IN_VMEM] * (1 + replicas),
        out_shape=shape(everyone, 1, 2 * size),
        scratch_shapes=[pltpu.VMEM((2 * size, LANES), jnp.float32)],
        compiler_params=params,
        name="gram_b",
    )(position, rows_a, *near, *far_b)
    gathered = lax.all_to_all(spread, ("dp", "tensor"), 0, 0, tiled=True)

    row_out = shape(owned_rows, columns)
    moment_out = shape(*first_moment_estimate.shape)
    updated_down_factor, updated_up_factor, moment_one, moment_two = pl.pallas_call(
        functools.partial(finish_kernel, replicas=replicas),
        out_shape=(row_out, row_out, moment_out, moment_out),
        compiler_params=params,
        name="finish",
    )(
        gathered,
        maps,
        *near,
        *far_a,
        *far_b,
        first_moment_estimate,
        second_moment_estimate,
        owned_down,
        owned_up,
    )
    return (input_grad, updated_down_factor, updated_up_factor, moment_one, moment_two)


def solution(mesh):
    placed = (
        P("dp", "tensor"),
        P("dp", "tensor"),
        P(None, "tensor"),
        P(None, "tensor"),
        P(None, "dp", "tensor"),
        P(None, "dp", "tensor"),
    )
    return jax.shard_map(
        body,
        mesh=mesh,
        in_specs=placed,
        out_specs=(
            P("dp", "tensor"),
            P("dp", "tensor"),
            P("dp", "tensor"),
            P(None, "dp", "tensor"),
            P(None, "dp", "tensor"),
        ),
        check_vma=False,
    )
```

```python
import functools

import jax
import jax.numpy as jnp
from jax import lax
from jax.experimental import pallas as pl
from jax.experimental.pallas import tpu as pltpu
from jax.sharding import PartitionSpec as P

SCALE = 2.0
NORM_EPS = 1e-06
LANES = 128
VMEM_LIMIT = 32 * 1024 * 1024
IN_VMEM = pl.BlockSpec(memory_space=pltpu.VMEM)
IN_HBM = pl.BlockSpec(memory_space=pltpu.HBM)
IN_SMEM = pl.BlockSpec(memory_space=pltpu.SMEM)


def other_of(block, axis, apart):
    route = [(here, here ^ apart) for here in range(lax.axis_size(axis))]
    return lax.ppermute(block, axis, route)


def butterfly_sum(block, axis, apart):
    other = jnp.zeros_like(block)
    while apart < lax.axis_size(axis):
        block = block + other
        other = other_of(block, axis, apart)
        apart *= 2
    return block, other


def pieces_of(factor, refs, replicas, owned):
    near = refs[: replicas // 2]
    far = refs[replicas // 2 : replicas]
    return [ref.at[factor * owned : (factor + 1) * owned] for ref in near] + list(far)


def inner_products(pieces, rows_ref, first, me):
    replicas = len(pieces)
    columns = pieces[0].shape[1]
    pairs = [(i, j) for i in range(replicas) for j in range(i, replicas)]
    sums = {}
    for start in range(0, columns, LANES):
        parts = [ref[:, start : start + LANES] for ref in pieces]
        for i, j in pairs:
            product = parts[i] * parts[j]
            sums[i, j] = sums[i, j] + product if start else product
    for i, j in pairs:
        row = jnp.sum(sums[i, j], axis=0, keepdims=True)
        one, two = i ^ me, j ^ me
        rows_ref[pl.ds(first + one * replicas + two, 1), :] = row
        if i != j:
            rows_ref[pl.ds(first + two * replicas + one, 1), :] = row


def tree_maps(maps_ref, me, replicas):
    size = replicas * replicas
    lanes = maps_ref.shape[1]
    source = lax.broadcasted_iota(jnp.int32, (lanes, lanes), 0)
    target = lax.broadcasted_iota(jnp.int32, (lanes, lanes), 1)
    for level in range(maps_ref.shape[0]):
        at = source ^ (me * replicas + me) if level == 0 else source
        same_factor = at // size == target // size
        left, right = at % size // replicas >> level, at % replicas >> level
        maps = []
        for group in (target % size // replicas >> level, target % replicas >> level):
            maps.append(same_factor & (left == group) & (right == group))
            maps.append(same_factor & (left == group) & (right == (group ^ 1)))
        maps.append(at == target)
        for place, chosen in enumerate(maps):
            maps_ref[level, :, place * lanes : (place + 1) * lanes] = jnp.where(
                chosen, 1.0, 0.0
            ).astype(maps_ref.dtype)


def mapped(values, map_ref, count):
    high = values.astype(jnp.bfloat16).astype(jnp.float32)
    middle = (values - high).astype(jnp.bfloat16).astype(jnp.float32)
    row = lax.broadcasted_iota(jnp.int32, values.shape, 0)
    parts = jnp.where(row == 0, high, jnp.where(row == 1, middle, values - high - middle))
    parts = jnp.where(row < 3, parts, 0.0).astype(jnp.bfloat16)
    lanes = values.shape[1]
    found = jnp.dot(
        parts, map_ref[:, : count * lanes], preferred_element_type=jnp.float32
    )
    found = jnp.broadcast_to(jnp.sum(found, axis=0, keepdims=True), found.shape)
    return [found[:, k * lanes : (k + 1) * lanes] for k in range(count)]


def tree_weights(gram, maps_ref):
    weights = jnp.ones_like(gram)
    for level in range(maps_ref.shape[0]):
        if level == 0:
            *terms, gram = mapped(gram, maps_ref.at[level], 5)
        else:
            terms = mapped(gram, maps_ref.at[level], 4)
        kept = []
        for norm, cross in (terms[:2], terms[2:]):
            norm = jnp.maximum(norm, 0.0)
            kept.append(1.0 - cross / (2.0 * (norm + NORM_EPS)))
        gram = gram * kept[0] * kept[1]
        weights = weights * kept[0]
    return weights


def first_gram_kernel(me_ref, down_ref, up_ref, *refs):
    *piece_refs, rows_ref, maps_ref, own_down_ref, own_up_ref, sems = refs
    replicas = len(piece_refs)
    owned = piece_refs[-1].shape[0]
    place = pl.ds(pl.multiple_of(me_ref[0] * owned, owned), owned)
    copies = [
        pltpu.make_async_copy(down_ref.at[place], own_down_ref, sems.at[0]),
        pltpu.make_async_copy(up_ref.at[place], own_up_ref, sems.at[1]),
    ]
    for copy in copies:
        copy.start()
    inner_products(pieces_of(0, piece_refs, replicas, owned), rows_ref, 0, me_ref[0])
    tree_maps(maps_ref, me_ref[0], replicas)
    for copy in copies:
        copy.wait()


def second_gram_kernel(me_ref, other_rows_ref, *refs):
    *piece_refs, spread_ref, rows_ref = refs
    replicas = len(piece_refs)
    owned = piece_refs[-1].shape[0]
    size = replicas * replicas
    rows_ref[:size, :] = other_rows_ref[...]
    inner_products(pieces_of(1, piece_refs, replicas, owned), rows_ref, size, me_ref[0])
    gram = jnp.sum(rows_ref[...].T, axis=0, keepdims=True)
    spread_ref[...] = jnp.broadcast_to(gram[None], spread_ref.shape)


def finish_kernel(gathered_ref, maps_ref, *refs, replicas):
    half = replicas // 2
    near, far_a, far_b = refs[:half], refs[half : 2 * half], refs[2 * half : 3 * half]
    first_ref, second_ref, down_ref, up_ref = refs[3 * half : 3 * half + 4]
    new_down_ref, new_up_ref, new_first_ref, new_second_ref = refs[3 * half + 4 :]
    gram = jnp.sum(gathered_ref[...], axis=0)
    gram = jnp.broadcast_to(gram, (16, gram.shape[1]))
    weights = tree_weights(gram, maps_ref)
    factors = ((far_a, down_ref, new_down_ref), (far_b, up_ref, new_up_ref))
    for factor, (far, old_ref, new_ref) in enumerate(factors):
        owned = old_ref.shape[0]
        combined = jnp.zeros(old_ref.shape, jnp.float32)
        for i, piece_ref in enumerate(pieces_of(factor, near + far, replicas, owned)):
            lane = (factor * replicas + i) * replicas
            combined += weights[:1, lane : lane + 1] * piece_ref[...]
        moment_one = 0.9 * first_ref[factor] + 0.1 * combined
        moment_two = 0.95 * second_ref[factor] + 0.05 * combined * combined
        new_first_ref[factor] = moment_one
        new_second_ref[factor] = moment_two
        change = 0.001 * moment_one / (jnp.sqrt(moment_two) + 1e-08)
        new_ref[...] = old_ref[...] - change


def body(
    tokens,
    cotangent,
    lowrank_down_factor,
    lowrank_up_factor,
    first_moment_estimate,
    second_moment_estimate,
):
    replicas = lax.axis_size("dp")
    everyone = replicas * lax.axis_size("tensor")
    half = replicas // 2
    rows, columns = tokens.shape
    rank = lowrank_down_factor.shape[0]
    owned_rows = first_moment_estimate.shape[1]
    size = replicas * replicas
    levels = replicas.bit_length() - 1
    me = lax.axis_index("dp")
    position = me.astype(jnp.int32).reshape(1)
    params = pltpu.CompilerParams(vmem_limit_bytes=VMEM_LIMIT)

    def shape(*dims, dtype=jnp.float32):
        return jax.ShapeDtypeStruct(dims, dtype)

    def projected(block, factor):
        return lax.dot_general(
            factor,
            block,
            (((1,), (1,)), ((), ())),
            preferred_element_type=jnp.float32,
        )

    def half_of(block, owner):
        start = owner // half * (half * owned_rows)
        return lax.dynamic_slice_in_dim(block, start, half * owned_rows, 0)

    def sent(block, apart):
        route = [(here, here ^ apart) for here in range(replicas)]
        return lax.ppermute(block, "dp", route)

    def rank_sums(addends):
        return (SCALE * (addends[0] + addends[1])).astype(jnp.bfloat16)

    def gradient(sums, block):
        return jnp.dot(sums, block, preferred_element_type=jnp.float32)

    def pieces_for(grad):
        return [
            lax.dynamic_slice_in_dim(
                grad, (me ^ k) % half * owned_rows, owned_rows, 0
            )
            for k in range(half)
        ]

    adapter_in = lowrank_down_factor.astype(jnp.bfloat16)
    adapter_out = lowrank_up_factor.astype(jnp.bfloat16)
    adapter_in = lax.optimization_barrier(adapter_in)
    upstream = projected(cotangent, adapter_out)
    hidden = projected(tokens, adapter_in)
    upstream = upstream + other_of(upstream, "tensor", 1)
    hidden = hidden + other_of(hidden, "tensor", 1)
    far_owner = (me + half) % replicas
    upstream_far = rank_sums(butterfly_sum(half_of(upstream, far_owner), "tensor", 2))
    far_a = pieces_for(gradient(upstream_far, tokens))
    rest = jnp.concatenate(
        [half_of(hidden, far_owner), half_of(hidden, me), half_of(upstream, me)]
    )
    for k in range(half):
        far_a[k] = sent(far_a[k], half + k)
    rest = rank_sums(butterfly_sum(rest, "tensor", 2))
    hidden, upstream_near = rest[:rank], rest[rank:]
    grad_b = gradient(hidden, cotangent)
    far_b = pieces_for(grad_b[: rank // 2])
    near_b = pieces_for(grad_b[rank // 2 :])
    near_a = pieces_for(gradient(upstream_near, tokens))
    near = [jnp.concatenate(pair) for pair in zip(near_a, near_b)]
    far_a[0], far_b[1] = lax.optimization_barrier((far_a[0], far_b[1]))
    far_a[1], far_b[2] = lax.optimization_barrier((far_a[1], far_b[2]))
    far_a[2], far_b[3] = lax.optimization_barrier((far_a[2], far_b[3]))
    for k in range(half):
        far_b[k] = sent(far_b[k], half + k)
    near = near[:1] + [sent(piece, k) for k, piece in enumerate(near) if k]

    far_b[0], upstream_near = lax.optimization_barrier((far_b[0], upstream_near))

    upstream = jnp.where(
        me < half,
        jnp.concatenate([upstream_near, upstream_far]),
        jnp.concatenate([upstream_far, upstream_near]),
    )
    input_grad = lax.dot_general(
        upstream,
        adapter_in,
        (((0,), (0,)), ((), ())),
        preferred_element_type=jnp.float32,
    )
    input_grad = input_grad.astype(jnp.bfloat16)
    near, input_grad = lax.optimization_barrier((near, input_grad))

    row_out = shape(owned_rows, columns)
    rows_a, maps, owned_down, owned_up = pl.pallas_call(
        first_gram_kernel,
        in_specs=[IN_SMEM] + [IN_HBM] * 2 + [IN_VMEM] * replicas,
        out_shape=[
            shape(size, LANES),
            shape(levels, 2 * size, 10 * size, dtype=jnp.bfloat16),
            row_out,
            row_out,
        ],
        scratch_shapes=[pltpu.SemaphoreType.DMA((2,))],
        compiler_params=params,
        name="gram_a",
    )(position, lowrank_down_factor, lowrank_up_factor, *near, *far_a)
    spread = pl.pallas_call(
        second_gram_kernel,
        in_specs=[IN_SMEM] + [IN_VMEM] * (1 + replicas),
        out_shape=shape(everyone, 1, 2 * size),
        scratch_shapes=[pltpu.VMEM((2 * size, LANES), jnp.float32)],
        compiler_params=params,
        name="gram_b",
    )(position, rows_a, *near, *far_b)
    gathered = lax.all_to_all(spread, ("dp", "tensor"), 0, 0, tiled=True)

    moment_out = shape(*first_moment_estimate.shape)
    updated_down_factor, updated_up_factor, moment_one, moment_two = pl.pallas_call(
        functools.partial(finish_kernel, replicas=replicas),
        out_shape=(row_out, row_out, moment_out, moment_out),
        compiler_params=params,
        name="finish",
    )(
        gathered,
        maps,
        *near,
        *far_a,
        *far_b,
        first_moment_estimate,
        second_moment_estimate,
        owned_down,
        owned_up,
    )
    return (input_grad, updated_down_factor, updated_up_factor, moment_one, moment_two)


def solution(mesh):
    placed = (
        P("dp", "tensor"),
        P("dp", "tensor"),
        P(None, "tensor"),
        P(None, "tensor"),
        P(None, "dp", "tensor"),
        P(None, "dp", "tensor"),
    )
    return jax.shard_map(
        body,
        mesh=mesh,
        in_specs=placed,
        out_specs=(
            P("dp", "tensor"),
            P("dp", "tensor"),
            P("dp", "tensor"),
            P(None, "dp", "tensor"),
            P(None, "dp", "tensor"),
        ),
        check_vma=False,
    )
```

```python
import functools

import jax
import jax.numpy as jnp
from jax import lax
from jax.experimental import pallas as pl
from jax.experimental.pallas import tpu as pltpu
from jax.sharding import PartitionSpec as P

SCALE = 2.0
NORM_EPS = 1e-06
LANES = 128
VMEM_LIMIT = 32 * 1024 * 1024
IN_VMEM = pl.BlockSpec(memory_space=pltpu.VMEM)
IN_HBM = pl.BlockSpec(memory_space=pltpu.HBM)
IN_SMEM = pl.BlockSpec(memory_space=pltpu.SMEM)


def other_of(block, axis, apart):
    route = [(here, here ^ apart) for here in range(lax.axis_size(axis))]
    return lax.ppermute(block, axis, route)


def butterfly_sum(block, axis, apart):
    other = jnp.zeros_like(block)
    while apart < lax.axis_size(axis):
        block = block + other
        other = other_of(block, axis, apart)
        apart *= 2
    return block, other


def pieces_of(factor, refs, replicas, owned):
    near = refs[: replicas // 2]
    far = refs[replicas // 2 : replicas]
    return [ref.at[factor * owned : (factor + 1) * owned] for ref in near] + list(far)


def inner_products(pieces, rows_ref, first, me):
    replicas = len(pieces)
    columns = pieces[0].shape[1]
    pairs = [(i, j) for i in range(replicas) for j in range(i, replicas)]
    sums = {}
    for start in range(0, columns, LANES):
        parts = [ref[:, start : start + LANES] for ref in pieces]
        for i, j in pairs:
            product = parts[i] * parts[j]
            sums[i, j] = sums[i, j] + product if start else product
    for i, j in pairs:
        row = jnp.sum(sums[i, j], axis=0, keepdims=True)
        one, two = i ^ me, j ^ me
        rows_ref[pl.ds(first + one * replicas + two, 1), :] = row
        if i != j:
            rows_ref[pl.ds(first + two * replicas + one, 1), :] = row


def tree_maps(maps_ref, me, replicas):
    size = replicas * replicas
    lanes = maps_ref.shape[1]
    source = lax.broadcasted_iota(jnp.int32, (lanes, lanes), 0)
    target = lax.broadcasted_iota(jnp.int32, (lanes, lanes), 1)
    for level in range(maps_ref.shape[0]):
        at = source ^ (me * replicas + me) if level == 0 else source
        same_factor = at // size == target // size
        left, right = at % size // replicas >> level, at % replicas >> level
        maps = []
        for group in (target % size // replicas >> level, target % replicas >> level):
            maps.append(same_factor & (left == group) & (right == group))
            maps.append(same_factor & (left == group) & (right == (group ^ 1)))
        maps.append(at == target)
        for place, chosen in enumerate(maps):
            maps_ref[level, :, place * lanes : (place + 1) * lanes] = jnp.where(
                chosen, 1.0, 0.0
            ).astype(maps_ref.dtype)


def mapped(values, map_ref, count):
    high = values.astype(jnp.bfloat16).astype(jnp.float32)
    middle = (values - high).astype(jnp.bfloat16).astype(jnp.float32)
    row = lax.broadcasted_iota(jnp.int32, values.shape, 0)
    parts = jnp.where(row == 0, high, jnp.where(row == 1, middle, values - high - middle))
    parts = jnp.where(row < 3, parts, 0.0).astype(jnp.bfloat16)
    lanes = values.shape[1]
    found = jnp.dot(
        parts, map_ref[:, : count * lanes], preferred_element_type=jnp.float32
    )
    found = jnp.broadcast_to(jnp.sum(found, axis=0, keepdims=True), found.shape)
    return [found[:, k * lanes : (k + 1) * lanes] for k in range(count)]


def tree_weights(gram, maps_ref):
    weights = jnp.ones_like(gram)
    for level in range(maps_ref.shape[0]):
        if level == 0:
            *terms, gram = mapped(gram, maps_ref.at[level], 5)
        else:
            terms = mapped(gram, maps_ref.at[level], 4)
        kept = []
        for norm, cross in (terms[:2], terms[2:]):
            norm = jnp.maximum(norm, 0.0)
            kept.append(1.0 - cross / (2.0 * (norm + NORM_EPS)))
        gram = gram * kept[0] * kept[1]
        weights = weights * kept[0]
    return weights


def first_gram_kernel(me_ref, down_ref, up_ref, *refs):
    *piece_refs, rows_ref, maps_ref, own_down_ref, own_up_ref, sems = refs
    replicas = len(piece_refs)
    owned = piece_refs[-1].shape[0]
    place = pl.ds(pl.multiple_of(me_ref[0] * owned, owned), owned)
    copies = [
        pltpu.make_async_copy(down_ref.at[place], own_down_ref, sems.at[0]),
        pltpu.make_async_copy(up_ref.at[place], own_up_ref, sems.at[1]),
    ]
    for copy in copies:
        copy.start()
    inner_products(pieces_of(0, piece_refs, replicas, owned), rows_ref, 0, me_ref[0])
    tree_maps(maps_ref, me_ref[0], replicas)
    for copy in copies:
        copy.wait()


def second_gram_kernel(me_ref, other_rows_ref, *refs):
    *piece_refs, spread_ref, rows_ref = refs
    replicas = len(piece_refs)
    owned = piece_refs[-1].shape[0]
    size = replicas * replicas
    rows_ref[:size, :] = other_rows_ref[...]
    inner_products(pieces_of(1, piece_refs, replicas, owned), rows_ref, size, me_ref[0])
    gram = jnp.sum(rows_ref[...].T, axis=0, keepdims=True)
    spread_ref[...] = jnp.broadcast_to(gram[None], spread_ref.shape)


def finish_kernel(gathered_ref, maps_ref, *refs, replicas):
    half = replicas // 2
    near, far_a, far_b = refs[:half], refs[half : 2 * half], refs[2 * half : 3 * half]
    first_ref, second_ref, down_ref, up_ref = refs[3 * half : 3 * half + 4]
    new_down_ref, new_up_ref, new_first_ref, new_second_ref = refs[3 * half + 4 :]
    gram = jnp.sum(gathered_ref[...], axis=0)
    gram = jnp.broadcast_to(gram, (16, gram.shape[1]))
    weights = tree_weights(gram, maps_ref)
    factors = ((far_a, down_ref, new_down_ref), (far_b, up_ref, new_up_ref))
    for factor, (far, old_ref, new_ref) in enumerate(factors):
        owned = old_ref.shape[0]
        combined = jnp.zeros(old_ref.shape, jnp.float32)
        for i, piece_ref in enumerate(pieces_of(factor, near + far, replicas, owned)):
            lane = (factor * replicas + i) * replicas
            combined += weights[:1, lane : lane + 1] * piece_ref[...]
        moment_one = 0.9 * first_ref[factor] + 0.1 * combined
        moment_two = 0.95 * second_ref[factor] + 0.05 * combined * combined
        new_first_ref[factor] = moment_one
        new_second_ref[factor] = moment_two
        change = 0.001 * moment_one / (jnp.sqrt(moment_two) + 1e-08)
        new_ref[...] = old_ref[...] - change


def body(
    tokens,
    cotangent,
    lowrank_down_factor,
    lowrank_up_factor,
    first_moment_estimate,
    second_moment_estimate,
):
    replicas = lax.axis_size("dp")
    everyone = replicas * lax.axis_size("tensor")
    half = replicas // 2
    rows, columns = tokens.shape
    rank = lowrank_down_factor.shape[0]
    owned_rows = first_moment_estimate.shape[1]
    size = replicas * replicas
    levels = replicas.bit_length() - 1
    me = lax.axis_index("dp")
    position = me.astype(jnp.int32).reshape(1)
    params = pltpu.CompilerParams(vmem_limit_bytes=VMEM_LIMIT)

    def shape(*dims, dtype=jnp.float32):
        return jax.ShapeDtypeStruct(dims, dtype)

    def projected(block, factor):
        return lax.dot_general(
            factor,
            block,
            (((1,), (1,)), ((), ())),
            preferred_element_type=jnp.float32,
        )

    def half_of(block, owner):
        start = owner // half * (half * owned_rows)
        return lax.dynamic_slice_in_dim(block, start, half * owned_rows, 0)

    def sent(block, apart):
        route = [(here, here ^ apart) for here in range(replicas)]
        return lax.ppermute(block, "dp", route)

    def rank_sums(addends):
        return (SCALE * (addends[0] + addends[1])).astype(jnp.bfloat16)

    def gradient(sums, block):
        return jnp.dot(sums, block, preferred_element_type=jnp.float32)

    def pieces_for(grad):
        return [
            lax.dynamic_slice_in_dim(
                grad, (me ^ k) % half * owned_rows, owned_rows, 0
            )
            for k in range(half)
        ]

    adapter_in = lowrank_down_factor.astype(jnp.bfloat16)
    adapter_out = lowrank_up_factor.astype(jnp.bfloat16)
    adapter_in = lax.optimization_barrier(adapter_in)
    upstream = projected(cotangent, adapter_out)
    hidden = projected(tokens, adapter_in)
    upstream = upstream + other_of(upstream, "tensor", 1)
    hidden = hidden + other_of(hidden, "tensor", 1)
    far_owner = (me + half) % replicas
    upstream_far = rank_sums(butterfly_sum(half_of(upstream, far_owner), "tensor", 2))
    far_a = pieces_for(gradient(upstream_far, tokens))
    rest = jnp.concatenate(
        [half_of(hidden, far_owner), half_of(hidden, me), half_of(upstream, me)]
    )
    for k in range(half):
        far_a[k] = sent(far_a[k], half + k)
    rest = rank_sums(butterfly_sum(rest, "tensor", 2))
    hidden, upstream_near = rest[:rank], rest[rank:]
    grad_b = gradient(hidden, cotangent)
    far_b = pieces_for(grad_b[: rank // 2])
    near_b = pieces_for(grad_b[rank // 2 :])
    near_a = pieces_for(gradient(upstream_near, tokens))
    near = [jnp.concatenate(pair) for pair in zip(near_a, near_b)]
    far_a[1], far_b[1] = lax.optimization_barrier((far_a[1], far_b[1]))
    far_a[2], far_b[2] = lax.optimization_barrier((far_a[2], far_b[2]))
    far_a[2], far_b[3] = lax.optimization_barrier((far_a[2], far_b[3]))
    far_a[0], near[1] = lax.optimization_barrier((far_a[0], near[1]))
    for k in (1, 2, 3):
        near[k] = sent(near[k], k)
    for k in range(half):
        far_b[k] = sent(far_b[k], half + k)
    far_b[0], upstream_near = lax.optimization_barrier((far_b[0], upstream_near))

    upstream = jnp.where(
        me < half,
        jnp.concatenate([upstream_near, upstream_far]),
        jnp.concatenate([upstream_far, upstream_near]),
    )
    input_grad = lax.dot_general(
        upstream,
        adapter_in,
        (((0,), (0,)), ((), ())),
        preferred_element_type=jnp.float32,
    )
    input_grad = input_grad.astype(jnp.bfloat16)
    near, input_grad = lax.optimization_barrier((near, input_grad))

    row_out = shape(owned_rows, columns)
    rows_a, maps, owned_down, owned_up = pl.pallas_call(
        first_gram_kernel,
        in_specs=[IN_SMEM] + [IN_HBM] * 2 + [IN_VMEM] * replicas,
        out_shape=[
            shape(size, LANES),
            shape(levels, 2 * size, 10 * size, dtype=jnp.bfloat16),
            row_out,
            row_out,
        ],
        scratch_shapes=[pltpu.SemaphoreType.DMA((2,))],
        compiler_params=params,
        name="gram_a",
    )(position, lowrank_down_factor, lowrank_up_factor, *near, *far_a)
    spread = pl.pallas_call(
        second_gram_kernel,
        in_specs=[IN_SMEM] + [IN_VMEM] * (1 + replicas),
        out_shape=shape(everyone, 1, 2 * size),
        scratch_shapes=[pltpu.VMEM((2 * size, LANES), jnp.float32)],
        compiler_params=params,
        name="gram_b",
    )(position, rows_a, *near, *far_b)
    gathered = lax.all_to_all(spread, ("dp", "tensor"), 0, 0, tiled=True)

    moment_out = shape(*first_moment_estimate.shape)
    updated_down_factor, updated_up_factor, moment_one, moment_two = pl.pallas_call(
        functools.partial(finish_kernel, replicas=replicas),
        out_shape=(row_out, row_out, moment_out, moment_out),
        compiler_params=params,
        name="finish",
    )(
        gathered,
        maps,
        *near,
        *far_a,
        *far_b,
        first_moment_estimate,
        second_moment_estimate,
        owned_down,
        owned_up,
    )
    return (input_grad, updated_down_factor, updated_up_factor, moment_one, moment_two)


def solution(mesh):
    placed = (
        P("dp", "tensor"),
        P("dp", "tensor"),
        P(None, "tensor"),
        P(None, "tensor"),
        P(None, "dp", "tensor"),
        P(None, "dp", "tensor"),
    )
    return jax.shard_map(
        body,
        mesh=mesh,
        in_specs=placed,
        out_specs=(
            P("dp", "tensor"),
            P("dp", "tensor"),
            P("dp", "tensor"),
            P(None, "dp", "tensor"),
            P(None, "dp", "tensor"),
        ),
        check_vma=False,
    )
```

```python
import functools

import jax
import jax.numpy as jnp
from jax import lax
from jax.experimental import pallas as pl
from jax.experimental.pallas import tpu as pltpu
from jax.sharding import PartitionSpec as P

SCALE = 2.0
NORM_EPS = 1e-06
LANES = 128
VMEM_LIMIT = 12 * 1024 * 1024
IN_VMEM = pl.BlockSpec(memory_space=pltpu.VMEM)
IN_HBM = pl.BlockSpec(memory_space=pltpu.HBM)
IN_SMEM = pl.BlockSpec(memory_space=pltpu.SMEM)


def other_of(block, axis, apart):
    route = [(here, here ^ apart) for here in range(lax.axis_size(axis))]
    return lax.ppermute(block, axis, route)


def butterfly_sum(block, axis, apart):
    other = jnp.zeros_like(block)
    while apart < lax.axis_size(axis):
        block = block + other
        other = other_of(block, axis, apart)
        apart *= 2
    return block, other


def pieces_of(factor, refs, replicas, owned):
    near = refs[: replicas // 2]
    far = refs[replicas // 2 : replicas]
    return [ref.at[factor * owned : (factor + 1) * owned] for ref in near] + list(far)


def inner_products(pieces, rows_ref, first, me):
    replicas = len(pieces)
    columns = pieces[0].shape[1]
    pairs = [(i, j) for i in range(replicas) for j in range(i, replicas)]
    sums = {}
    for start in range(0, columns, LANES):
        parts = [ref[:, start : start + LANES] for ref in pieces]
        for i, j in pairs:
            product = parts[i] * parts[j]
            sums[i, j] = sums[i, j] + product if start else product
    for i, j in pairs:
        row = jnp.sum(sums[i, j], axis=0, keepdims=True)
        one, two = i ^ me, j ^ me
        rows_ref[pl.ds(first + one * replicas + two, 1), :] = row
        if i != j:
            rows_ref[pl.ds(first + two * replicas + one, 1), :] = row


def tree_maps(maps_ref, me, replicas):
    size = replicas * replicas
    lanes = maps_ref.shape[1]
    source = lax.broadcasted_iota(jnp.int32, (lanes, lanes), 0)
    target = lax.broadcasted_iota(jnp.int32, (lanes, lanes), 1)
    for level in range(maps_ref.shape[0]):
        at = source ^ (me * replicas + me) if level == 0 else source
        same_factor = at // size == target // size
        left, right = at % size // replicas >> level, at % replicas >> level
        maps = []
        for group in (target % size // replicas >> level, target % replicas >> level):
            maps.append(same_factor & (left == group) & (right == group))
            maps.append(same_factor & (left == group) & (right == (group ^ 1)))
        maps.append(at == target)
        for place, chosen in enumerate(maps):
            maps_ref[level, :, place * lanes : (place + 1) * lanes] = jnp.where(
                chosen, 1.0, 0.0
            ).astype(maps_ref.dtype)


def mapped(values, map_ref, count):
    high = values.astype(jnp.bfloat16).astype(jnp.float32)
    middle = (values - high).astype(jnp.bfloat16).astype(jnp.float32)
    row = lax.broadcasted_iota(jnp.int32, values.shape, 0)
    parts = jnp.where(row == 0, high, jnp.where(row == 1, middle, values - high - middle))
    parts = jnp.where(row < 3, parts, 0.0).astype(jnp.bfloat16)
    lanes = values.shape[1]
    found = jnp.dot(
        parts, map_ref[:, : count * lanes], preferred_element_type=jnp.float32
    )
    found = jnp.broadcast_to(jnp.sum(found, axis=0, keepdims=True), found.shape)
    return [found[:, k * lanes : (k + 1) * lanes] for k in range(count)]


def tree_weights(gram, maps_ref):
    weights = jnp.ones_like(gram)
    for level in range(maps_ref.shape[0]):
        if level == 0:
            *terms, gram = mapped(gram, maps_ref.at[level], 5)
        else:
            terms = mapped(gram, maps_ref.at[level], 4)
        kept = []
        for norm, cross in (terms[:2], terms[2:]):
            norm = jnp.maximum(norm, 0.0)
            kept.append(1.0 - cross / (2.0 * (norm + NORM_EPS)))
        gram = gram * kept[0] * kept[1]
        weights = weights * kept[0]
    return weights


def first_gram_kernel(me_ref, down_ref, up_ref, *refs):
    *piece_refs, rows_ref, maps_ref, own_down_ref, own_up_ref, sems = refs
    replicas = len(piece_refs)
    owned = piece_refs[-1].shape[0]
    place = pl.ds(pl.multiple_of(me_ref[0] * owned, owned), owned)
    copies = [
        pltpu.make_async_copy(down_ref.at[place], own_down_ref, sems.at[0]),
        pltpu.make_async_copy(up_ref.at[place], own_up_ref, sems.at[1]),
    ]
    for copy in copies:
        copy.start()
    inner_products(pieces_of(0, piece_refs, replicas, owned), rows_ref, 0, me_ref[0])
    tree_maps(maps_ref, me_ref[0], replicas)
    for copy in copies:
        copy.wait()


def second_gram_kernel(me_ref, other_rows_ref, *refs):
    *piece_refs, spread_ref, rows_ref = refs
    replicas = len(piece_refs)
    owned = piece_refs[-1].shape[0]
    size = replicas * replicas
    rows_ref[:size, :] = other_rows_ref[...]
    inner_products(pieces_of(1, piece_refs, replicas, owned), rows_ref, size, me_ref[0])
    gram = jnp.sum(rows_ref[...].T, axis=0, keepdims=True)
    spread_ref[...] = jnp.broadcast_to(gram[None], spread_ref.shape)


def finish_kernel(gathered_ref, maps_ref, *refs, replicas):
    half = replicas // 2
    near, far_a, far_b = refs[:half], refs[half : 2 * half], refs[2 * half : 3 * half]
    first_ref, second_ref, down_ref, up_ref = refs[3 * half : 3 * half + 4]
    new_down_ref, new_up_ref, new_first_ref, new_second_ref = refs[3 * half + 4 :]
    gram = jnp.sum(gathered_ref[...], axis=0)
    gram = jnp.broadcast_to(gram, (16, gram.shape[1]))
    weights = tree_weights(gram, maps_ref)
    factors = ((far_a, down_ref, new_down_ref), (far_b, up_ref, new_up_ref))
    for factor, (far, old_ref, new_ref) in enumerate(factors):
        owned = old_ref.shape[0]
        combined = jnp.zeros(old_ref.shape, jnp.float32)
        for i, piece_ref in enumerate(pieces_of(factor, near + far, replicas, owned)):
            lane = (factor * replicas + i) * replicas
            combined += weights[:1, lane : lane + 1] * piece_ref[...]
        moment_one = 0.9 * first_ref[factor] + 0.1 * combined
        moment_two = 0.95 * second_ref[factor] + 0.05 * combined * combined
        new_first_ref[factor] = moment_one
        new_second_ref[factor] = moment_two
        change = 0.001 * moment_one / (jnp.sqrt(moment_two) + 1e-08)
        new_ref[...] = old_ref[...] - change


def body(
    tokens,
    cotangent,
    lowrank_down_factor,
    lowrank_up_factor,
    first_moment_estimate,
    second_moment_estimate,
):
    replicas = lax.axis_size("dp")
    everyone = replicas * lax.axis_size("tensor")
    half = replicas // 2
    rows, columns = tokens.shape
    rank = lowrank_down_factor.shape[0]
    owned_rows = first_moment_estimate.shape[1]
    size = replicas * replicas
    levels = replicas.bit_length() - 1
    me = lax.axis_index("dp")
    position = me.astype(jnp.int32).reshape(1)
    params = pltpu.CompilerParams(vmem_limit_bytes=VMEM_LIMIT)

    def shape(*dims, dtype=jnp.float32):
        return jax.ShapeDtypeStruct(dims, dtype)

    def projected(block, factor):
        return lax.dot_general(
            factor,
            block,
            (((1,), (1,)), ((), ())),
            preferred_element_type=jnp.float32,
        )

    def half_of(block, owner):
        start = owner // half * (half * owned_rows)
        return lax.dynamic_slice_in_dim(block, start, half * owned_rows, 0)

    def sent(block, apart):
        route = [(here, here ^ apart) for here in range(replicas)]
        return lax.ppermute(block, "dp", route)

    def rank_sums(addends):
        return (SCALE * (addends[0] + addends[1])).astype(jnp.bfloat16)

    def gradient(sums, block):
        return jnp.dot(sums, block, preferred_element_type=jnp.float32)

    def pieces_for(grad):
        return [
            lax.dynamic_slice_in_dim(
                grad, (me ^ k) % half * owned_rows, owned_rows, 0
            )
            for k in range(half)
        ]

    adapter_in = lowrank_down_factor.astype(jnp.bfloat16)
    adapter_out = lowrank_up_factor.astype(jnp.bfloat16)
    adapter_in = lax.optimization_barrier(adapter_in)
    upstream = projected(cotangent, adapter_out)
    hidden = projected(tokens, adapter_in)
    upstream = upstream + other_of(upstream, "tensor", 1)
    hidden = hidden + other_of(hidden, "tensor", 1)
    far_owner = (me + half) % replicas
    upstream_far = rank_sums(butterfly_sum(half_of(upstream, far_owner), "tensor", 2))
    far_a = pieces_for(gradient(upstream_far, tokens))
    rest = jnp.concatenate(
        [half_of(hidden, far_owner), half_of(hidden, me), half_of(upstream, me)]
    )
    for k in range(half):
        far_a[k] = sent(far_a[k], half + k)
    rest = rank_sums(butterfly_sum(rest, "tensor", 2))
    hidden, upstream_near = rest[:rank], rest[rank:]
    grad_b = gradient(hidden, cotangent)
    far_b = pieces_for(grad_b[: rank // 2])
    near_a = pieces_for(gradient(upstream_near, tokens))
    near_b = pieces_for(grad_b[rank // 2 :])
    near = [jnp.concatenate(pair) for pair in zip(near_a, near_b)]
    far_a[1], far_b[1] = lax.optimization_barrier((far_a[1], far_b[1]))
    far_a[2], far_b[2] = lax.optimization_barrier((far_a[2], far_b[2]))
    far_a[2], far_b[3] = lax.optimization_barrier((far_a[2], far_b[3]))
    far_a[0], near[1] = lax.optimization_barrier((far_a[0], near[1]))
    for k in (1, 2, 3):
        near[k] = sent(near[k], k)
    for k in range(half):
        far_b[k] = sent(far_b[k], half + k)
    far_b[0], upstream_near = lax.optimization_barrier((far_b[0], upstream_near))

    upstream = jnp.where(
        me < half,
        jnp.concatenate([upstream_near, upstream_far]),
        jnp.concatenate([upstream_far, upstream_near]),
    )
    input_grad = lax.dot_general(
        upstream,
        adapter_in,
        (((0,), (0,)), ((), ())),
        preferred_element_type=jnp.float32,
    )
    input_grad = input_grad.astype(jnp.bfloat16)
    near, input_grad = lax.optimization_barrier((near, input_grad))

    row_out = shape(owned_rows, columns)
    rows_a, maps, owned_down, owned_up = pl.pallas_call(
        first_gram_kernel,
        in_specs=[IN_SMEM] + [IN_HBM] * 2 + [IN_VMEM] * replicas,
        out_shape=[
            shape(size, LANES),
            shape(levels, 2 * size, 10 * size, dtype=jnp.bfloat16),
            row_out,
            row_out,
        ],
        scratch_shapes=[pltpu.SemaphoreType.DMA((2,))],
        compiler_params=params,
        name="gram_a",
    )(position, lowrank_down_factor, lowrank_up_factor, *near, *far_a)
    spread = pl.pallas_call(
        second_gram_kernel,
        in_specs=[IN_SMEM] + [IN_VMEM] * (1 + replicas),
        out_shape=shape(everyone, 1, 2 * size),
        scratch_shapes=[pltpu.VMEM((2 * size, LANES), jnp.float32)],
        compiler_params=params,
        name="gram_b",
    )(position, rows_a, *near, *far_b)
    gathered = lax.all_to_all(spread, ("dp", "tensor"), 0, 0, tiled=True)

    moment_out = shape(*first_moment_estimate.shape)
    updated_down_factor, updated_up_factor, moment_one, moment_two = pl.pallas_call(
        functools.partial(finish_kernel, replicas=replicas),
        out_shape=(row_out, row_out, moment_out, moment_out),
        compiler_params=params,
        name="finish",
    )(
        gathered,
        maps,
        *near,
        *far_a,
        *far_b,
        first_moment_estimate,
        second_moment_estimate,
        owned_down,
        owned_up,
    )
    return (input_grad, updated_down_factor, updated_up_factor, moment_one, moment_two)


def solution(mesh):
    placed = (
        P("dp", "tensor"),
        P("dp", "tensor"),
        P(None, "tensor"),
        P(None, "tensor"),
        P(None, "dp", "tensor"),
        P(None, "dp", "tensor"),
    )
    return jax.shard_map(
        body,
        mesh=mesh,
        in_specs=placed,
        out_specs=(
            P("dp", "tensor"),
            P("dp", "tensor"),
            P("dp", "tensor"),
            P(None, "dp", "tensor"),
            P(None, "dp", "tensor"),
        ),
        check_vma=False,
    )
```
